32 devices in a mesh: seq: 4 (over y, x), chan: 8 (over z, core).
Axes of the slice: x: 2, y: 2, z: 4, core: 2. Of those that a mesh axis runs over, the one named last changes fastest.
Arguments:
- tokens_in: float32 [32768, 1024], P(('seq', 'chan')), may hold values from -6 to 6
- ln_gain: bfloat16 [2, 2, 1024], P(None, None, 'chan'), may hold values from 0.5 to 1.5
- ln_bias: bfloat16 [2, 2, 1024], P(None, None, 'chan'), may hold values from -3 to 3
- in_weight: bfloat16 [2, 1024, 3072], P(None, 'chan'), may hold values from -0.1875 to 0.1875
- short_weight: float32 [2, 3, 3, 1024], P(None, None, None, 'chan'), may hold values from -3 to 3
- filter_first: float32 [2, 33, 64], replicated, may hold values from -2 to 2
- filter_mid: float32 [2, 64, 64], replicated, may hold values from -1.5 to 1.5
- filter_last: float32 [2, 64, 1024], P(None, None, 'chan'), may hold values from -0.015625 to 0.015625
- conv_bias: float32 [2, 1024], P(None, 'chan'), may hold values from -4 to 4
- out_weight: bfloat16 [2, 1024, 1024], P(None, 'chan'), may hold values from -0.1875 to 0.1875
- up_weight: bfloat16 [2, 1024, 4096], P(None, 'chan'), may hold values from -0.1875 to 0.1875
- down_weight: bfloat16 [2, 4096, 1024], P(None, 'chan'), may hold values from -0.09375 to 0.09375
- group_kind: int32 [8], replicated, may hold values from 0 to 1, as said below
- filt_len: int32 [8], replicated, may hold values from 1024 to 4096, as said below
- decay_win: int32 [8], replicated, may hold values from 256 to 2048, as said below
- cotangent: float32 [32768, 1024], P(('seq', 'chan')), may hold values from -6 to 6
Outputs:
- tokens_out: float32 [32768, 1024], P(('seq', 'chan'))
- grad_tokens: float32 [32768, 1024], P(('seq', 'chan'))
- grad_ln_gain: float32 [2, 2, 1024], P(None, None, 'chan')
- grad_ln_bias: float32 [2, 2, 1024], P(None, None, 'chan')
- grad_in_weight: float32 [2, 1024, 3072], P(None, 'chan')
- grad_short_weight: float32 [2, 3, 3, 1024], P(None, None, None, 'chan')
- grad_filter_first: float32 [2, 33, 64], replicated
- grad_filter_mid: float32 [2, 64, 64], replicated
- grad_filter_last: float32 [2, 64, 1024], P(None, None, 'chan')
- grad_conv_bias: float32 [2, 1024], P(None, 'chan')
- grad_out_weight: float32 [2, 1024, 1024], P(None, 'chan')
- grad_up_weight: float32 [2, 1024, 4096], P(None, 'chan')
- grad_down_weight: float32 [2, 4096, 1024], P(None, 'chan')
The draws below stay inside these ranges and needn't reach their ends.
Inputs may be any that keep to these rules, and one draw needn't show every extreme that they name: `group_kind`: exactly 4 groups are 1; groups 2 m and 2 m + 1 are alike. `filt_len`: at least 2048 where group_kind is 1, at most 2048 where it is 0. `decay_win`: from 512 where group_kind is 1, at most 1024 where it is 0.
All inputs are finite; a program needn't handle non-finite values.
Results may differ from the reference program's by a relative error of at most 0.023.
Values may be sent and summed in bfloat16 or wider, within the bound.
A program may use at most 1 GiB of HBM per device.

```python
import jax
import jax.numpy as jnp
from jax import lax

D = 1024
FF = 4096
FILT_HID = 64
FILT_IN = 33
LAYERS = 2
SHORT = 2048
GROUP = 4096
GROUPS = 8
ROWS = 32768


def member_ranking(key):
    ranking = jax.random.permutation(key, jnp.arange(GROUPS // 2, dtype=jnp.int32))
    members = jnp.arange(GROUPS, dtype=jnp.int32) // 2
    return ranking[members]


def draw_group_kind(key, part):
    ranking = member_ranking(key)
    return (ranking < GROUPS // 4).astype(jnp.int32)


def draw_filt_len(key, part):
    ranking = member_ranking(key)
    first_of_pair = jnp.arange(GROUPS, dtype=jnp.int32) % 2 == 0
    key = jax.random.fold_in(key, 11)
    spread_draw = jax.random.randint(key, (GROUPS,), 0, 1 << 20, dtype=jnp.int32)
    long_len = GROUP // 2 + spread_draw % (GROUP // 2 + 1)
    short_len = SHORT // 2 + spread_draw % (SHORT // 2 + 1)
    values = jnp.where(ranking < GROUPS // 4, long_len, short_len)
    values = jnp.where((ranking == 0) & first_of_pair, GROUP, values)
    return jnp.where((ranking == GROUPS // 4) & first_of_pair, SHORT // 2, values).astype(jnp.int32)


def draw_decay_win(key, part):
    ranking = member_ranking(key)
    first_of_pair = jnp.arange(GROUPS, dtype=jnp.int32) % 2 == 0
    key = jax.random.fold_in(key, 13)
    spread_draw = jax.random.randint(key, (GROUPS,), 0, 1 << 20, dtype=jnp.int32)
    long_win = GROUP // 8 + spread_draw % (GROUP // 2 - GROUP // 8 + 1)
    short_win = SHORT // 8 + spread_draw % (SHORT // 2 - SHORT // 8 + 1)
    values = jnp.where(ranking < GROUPS // 4, long_win, short_win)
    values = jnp.where((ranking == 0) & first_of_pair, GROUP // 2, values)
    return jnp.where((ranking == GROUPS // 4) & first_of_pair, SHORT // 8, values).astype(jnp.int32)


def shard_levels(key, dims, split, smallest, largest):
    loudness = 1.0
    for dim, shards_of in split:
        draws = jax.random.uniform(jax.random.fold_in(jax.random.fold_in(key, 6), dim), (shards_of,), jnp.float32, smallest / len(split), largest / len(split))
        loudness = loudness * jnp.repeat(jnp.exp(draws), dims[dim] // shards_of).reshape((-1,) + (1,) * (len(dims) - 1 - dim))
    return loudness


def scatter_about(key, shape, scale, limit, pieces=(), held_as=jnp.bfloat16):
    values = jax.random.normal(key, shape, jnp.float32) * scale
    if len(pieces) > 0:
        values = shard_levels(key, shape, pieces, -0.22, 0.18) * values
    return jnp.clip(values, min=-limit, max=limit).astype(held_as)


def setup_inputs(seed: int = 0) -> dict:
    splits = jax.random.split(jax.random.key(seed), 17)
    tokens_in = scatter_about(splits[0], (ROWS, D), 1.0, 6.0, ((0, 32),), jnp.float32)
    ln_gain = jnp.clip(1.0 + 0.1 * jax.random.normal(splits[1], (LAYERS, 2, D), jnp.float32), 0.5, 1.5).astype(jnp.bfloat16)
    ln_bias = scatter_about(splits[2], (LAYERS, 2, D), 0.3, 3.0, ((2, 8),))
    in_weight = scatter_about(splits[3], (LAYERS, D, 3 * D), D ** -0.5, 0.1875, ((1, 8),))
    short_weight = scatter_about(splits[4], (LAYERS, 3, 3, D), 0.6, 3.0, ((3, 8),), jnp.float32)
    filter_first = scatter_about(splits[5], (LAYERS, FILT_IN, FILT_HID), 8 ** -0.5, 2.0, (), jnp.float32)
    filter_mid = scatter_about(splits[6], (LAYERS, FILT_HID, FILT_HID), 16 ** -0.5, 1.5, (), jnp.float32)
    filter_last = scatter_about(splits[7], (LAYERS, FILT_HID, D), (FILT_HID * SHORT) ** -0.5, 0.015625, ((2, 8),), jnp.float32)
    conv_bias = scatter_about(splits[8], (LAYERS, D), 1.0, 4.0, ((1, 8),), jnp.float32)
    out_weight = scatter_about(splits[9], (LAYERS, D, D), D ** -0.5, 0.1875, ((1, 8),))
    up_weight = scatter_about(splits[10], (LAYERS, D, FF), D ** -0.5, 0.1875, ((1, 8),))
    down_weight = scatter_about(splits[11], (LAYERS, FF, D), FF ** -0.5, 0.09375, ((1, 8),))
    group_kind = draw_group_kind(jax.random.fold_in(splits[16], 71), 0)
    filt_len = draw_filt_len(jax.random.fold_in(splits[16], 71), 0)
    decay_win = draw_decay_win(jax.random.fold_in(splits[16], 71), 0)
    cotangent = scatter_about(splits[15], (ROWS, D), 1.0, 6.0, ((0, 32),), jnp.float32)
    return {"tokens_in": tokens_in, "ln_gain": ln_gain, "ln_bias": ln_bias, "in_weight": in_weight, "short_weight": short_weight, "filter_first": filter_first, "filter_mid": filter_mid, "filter_last": filter_last, "conv_bias": conv_bias, "out_weight": out_weight, "up_weight": up_weight, "down_weight": down_weight, "group_kind": group_kind, "filt_len": filt_len, "decay_win": decay_win, "cotangent": cotangent}


HIGHEST = lax.Precision.HIGHEST

@jax.custom_vjp
def low(v):
    return lax.optimization_barrier(v.astype(jnp.bfloat16)).astype(jnp.float32)

@jax.custom_vjp
def low_back(v):
    return v

def low_keep(v):
    return (low(v), None)

def low_pass(kept, grad):
    return (grad,)

def back_keep(v):
    return (v, None)

def back_low(kept, grad):
    return (low(grad),)
low.defvjp(low_keep, low_pass)
low_back.defvjp(back_keep, back_low)

def matmul(left, right):
    return jnp.dot(left, right, precision=HIGHEST, preferred_element_type=jnp.float32)

def layer_norm(values, norm_gain, norm_bias):
    average = lax.optimization_barrier(jnp.mean(values, axis=-1, keepdims=True))
    centred = values - average
    variance = lax.optimization_barrier(jnp.mean(centred * centred, axis=-1, keepdims=True))
    return centred * lax.rsqrt(variance + 1e-05) * norm_gain + norm_bias

def position_features(positions, length):
    fraction = positions / length
    frequency = jnp.arange(1, 17, dtype=jnp.float32)
    angles = 2.0 * jnp.pi * fraction[:, None] * frequency[None, :]
    return jnp.concatenate([fraction[:, None], jnp.cos(angles), jnp.sin(angles)], axis=1)

def filter_values(features, first_layer, middle, last_layer):
    hidden = jnp.sin(matmul(features, first_layer))
    hidden = jnp.sin(matmul(hidden, middle))
    return matmul(hidden, last_layer)

def short_mix(projected, tap_weights, doc_pos):
    summed = tap_weights[0][None] * projected
    for lag_count in (1, 2):
        shifted = jnp.concatenate([jnp.zeros((lag_count,) + projected.shape[1:], jnp.float32), projected[:-lag_count]], axis=0)
        summed = summed + tap_weights[lag_count][None] * shifted * (doc_pos >= lag_count).astype(jnp.float32)[:, None, None]
    return summed

def long_conv(signal, kernel, kind_here):
    length, width = signal.shape
    whole = jnp.fft.irfft(jnp.fft.rfft(signal, n=2 * length, axis=0) * jnp.fft.rfft(kernel, n=2 * length, axis=0), n=2 * length, axis=0)[:length]
    blocks = signal.reshape(length // SHORT, SHORT, width)
    spectrum = jnp.fft.rfft(kernel[:SHORT], n=2 * SHORT, axis=0)
    parted = jnp.fft.irfft(jnp.fft.rfft(blocks, n=2 * SHORT, axis=1) * spectrum[None], n=2 * SHORT, axis=1)[:, :SHORT]
    return jnp.where(kind_here == 1, whole, parted.reshape(length, width))

def mixer(projected, raw_filter, tap_weights, conv_shift, kind_here, stop_here, span_here, decay_rates):
    length = projected.shape[0]
    offsets = jnp.arange(length, dtype=jnp.int32)
    doc_pos = jnp.where(kind_here == 1, offsets, offsets % SHORT)
    shorted = short_mix(projected, tap_weights, doc_pos)
    signal = shorted[:, 0] * shorted[:, 2]
    damping = jnp.exp(-offsets.astype(jnp.float32)[:, None] * decay_rates[None, :] / span_here.astype(jnp.float32))
    inside = (offsets < stop_here).astype(jnp.float32)[:, None]
    kernel = raw_filter * damping * inside
    mixed_out = long_conv(signal, kernel, kind_here) + conv_shift[None, :] * signal
    return shorted[:, 1] * mixed_out

def forward(tokens_in, ln_gain, ln_bias, in_weight, short_weight, filter_first, filter_mid, filter_last, conv_bias, out_weight, up_weight, down_weight, group_kind, filt_len, decay_win):
    row_total = tokens_in.shape[0]
    features = position_features(jnp.arange(GROUP, dtype=jnp.float32), GROUP)
    channel_pos = jnp.arange(D, dtype=jnp.float32)
    decay_rates = jnp.exp(jnp.log(0.3) + jnp.log(100.0) * channel_pos / (D - 1))
    stream = tokens_in
    for layer_index in range(LAYERS):
        normed = low(layer_norm(stream, ln_gain[layer_index, 0], ln_bias[layer_index, 0]))
        projected = low(low_back(matmul(normed, in_weight[layer_index])))
        projected = projected.reshape(GROUPS, GROUP, 3, D)
        raw_filter = low(filter_values(features, filter_first[layer_index], filter_mid[layer_index], filter_last[layer_index]))
        mixed_out = jax.vmap(mixer, in_axes=(0, None, None, None, 0, 0, 0, None))(projected, raw_filter, short_weight[layer_index], conv_bias[layer_index], group_kind, filt_len, decay_win, decay_rates)
        gated = low(low_back(mixed_out.reshape(row_total, D)))
        stream = stream + low_back(matmul(gated, out_weight[layer_index]))
        normed = low(layer_norm(stream, ln_gain[layer_index, 1], ln_bias[layer_index, 1]))
        hidden = low(jax.nn.gelu(low_back(matmul(normed, up_weight[layer_index])), approximate=False))
        stream = stream + low_back(matmul(hidden, down_weight[layer_index]))
    return stream

def reference(tokens_in, ln_gain, ln_bias, in_weight, short_weight, filter_first, filter_mid, filter_last, conv_bias, out_weight, up_weight, down_weight, group_kind, filt_len, decay_win, cotangent):
    floats = (tokens_in.astype(jnp.float32), ln_gain.astype(jnp.float32), ln_bias.astype(jnp.float32), in_weight.astype(jnp.float32), short_weight.astype(jnp.float32), filter_first.astype(jnp.float32), filter_mid.astype(jnp.float32), filter_last.astype(jnp.float32), conv_bias.astype(jnp.float32), out_weight.astype(jnp.float32), up_weight.astype(jnp.float32), down_weight.astype(jnp.float32))

    def wrapped(*values):
        return forward(*values, group_kind, filt_len, decay_win)
    result, pullback = jax.vjp(wrapped, *floats)
    grads = pullback(cotangent.astype(jnp.float32))
    return (result, grads[0], grads[1], grads[2], grads[3], grads[4], grads[5], grads[6], grads[7], grads[8], grads[9], grads[10], grads[11])
```

```python
import functools
import math

import jax
import jax.numpy as jnp
import ml_dtypes
import numpy as np
from jax import lax
from jax.experimental import pallas as pl
from jax.experimental.pallas import tpu as pltpu
from jax.sharding import Mesh
from jax.sharding import PartitionSpec as P

LAYERS = 2
SHORT = 2048
BLOCK = 512
HALF = BLOCK // 2
TILE = 256
EDGE = 16
STRIP = 128
MIB = 1 << 20
F32 = jnp.float32
BF16 = jnp.bfloat16
LIGHT = pl.CostEstimate(flops=1000, bytes_accessed=1000, transcendentals=0)


HIGHEST = lax.Precision.HIGHEST


def precise_dot(left, right):
    return jnp.dot(left, right, precision=HIGHEST, preferred_element_type=jnp.float32)


def dot_lead(left, right):
    return lax.dot_general(
        left, right, (((0,), (0,)), ((), ())), preferred_element_type=jnp.float32
    )


def dot_trail(left, right):
    return lax.dot_general(
        left, right, (((1,), (1,)), ((), ())), preferred_element_type=jnp.float32
    )


def dot_cross(left, right):
    return lax.dot_general(
        left, right, (((0,), (1,)), ((), ())), preferred_element_type=jnp.float32
    )


def layer_norm(values, norm_gain, norm_bias):
    average = jnp.mean(values, axis=-1, keepdims=True)
    centred = values - average
    variance = jnp.mean(centred * centred, axis=-1, keepdims=True)
    return centred * lax.rsqrt(variance + 1e-05) * norm_gain + norm_bias


def position_features(positions, length):
    fraction = positions / length
    frequency = jnp.arange(1, 17, dtype=jnp.float32)
    angles = 2.0 * jnp.pi * fraction[:, None] * frequency[None, :]
    return jnp.concatenate([fraction[:, None], jnp.cos(angles), jnp.sin(angles)], axis=1)


def filter_columns(features, first_layer, middle, last_layer):
    hidden = jnp.sin(precise_dot(features, first_layer))
    hidden = jnp.sin(precise_dot(hidden, middle))
    return lax.dot_general(
        last_layer,
        hidden,
        (((0,), (1,)), ((), ())),
        precision=HIGHEST,
        preferred_element_type=jnp.float32,
    )


def angle_table(row_count, col_count, modulus):
    product = (
        jnp.arange(row_count, dtype=jnp.int32)[:, None]
        * jnp.arange(col_count, dtype=jnp.int32)[None, :]
        % modulus
    )
    angles = product.astype(jnp.float32) * (2.0 * math.pi / modulus)
    return (jnp.cos(angles), jnp.sin(angles))


def forward_dft(signal):
    length = signal.shape[-1]
    inner_size = 128
    outer_size = length // inner_size
    shaped = signal.reshape(signal.shape[:-1] + (outer_size, inner_size))
    cos_outer, sin_outer = angle_table(outer_size, outer_size, outer_size)
    cos_twist, sin_twist = angle_table(outer_size, inner_size, length)
    cos_inner, sin_inner = angle_table(inner_size, inner_size, inner_size)
    real_part = jnp.einsum("...ab,ak->...kb", shaped, cos_outer, precision=HIGHEST)
    imag_part = -jnp.einsum("...ab,ak->...kb", shaped, sin_outer, precision=HIGHEST)
    twist_real = real_part * cos_twist + imag_part * sin_twist
    twist_imag = imag_part * cos_twist - real_part * sin_twist
    out_real = jnp.einsum("...kb,bq->...kq", twist_real, cos_inner, precision=HIGHEST) + jnp.einsum(
        "...kb,bq->...kq", twist_imag, sin_inner, precision=HIGHEST
    )
    out_imag = jnp.einsum("...kb,bq->...kq", twist_imag, cos_inner, precision=HIGHEST) - jnp.einsum(
        "...kb,bq->...kq", twist_real, sin_inner, precision=HIGHEST
    )
    return (out_real, out_imag)


def inverse_dft(real_part, imag_part):
    outer_size = real_part.shape[-2]
    inner_size = real_part.shape[-1]
    length = outer_size * inner_size
    cos_outer, sin_outer = angle_table(outer_size, outer_size, outer_size)
    cos_twist, sin_twist = angle_table(outer_size, inner_size, length)
    cos_inner, sin_inner = angle_table(inner_size, inner_size, inner_size)
    step_real = jnp.einsum("...kq,qn->...kn", real_part, cos_inner, precision=HIGHEST) - jnp.einsum(
        "...kq,qn->...kn", imag_part, sin_inner, precision=HIGHEST
    )
    step_imag = jnp.einsum("...kq,qn->...kn", real_part, sin_inner, precision=HIGHEST) + jnp.einsum(
        "...kq,qn->...kn", imag_part, cos_inner, precision=HIGHEST
    )
    twist_real = step_real * cos_twist - step_imag * sin_twist
    twist_imag = step_real * sin_twist + step_imag * cos_twist
    result = jnp.einsum("...kn,ka->...an", twist_real, cos_outer, precision=HIGHEST) - jnp.einsum(
        "...kn,ka->...an", twist_imag, sin_outer, precision=HIGHEST
    )
    return result.reshape(result.shape[:-2] + (length,)) / length


def blocked_conv(signal, kernel, long_flag):
    chan_width, length = signal.shape
    block_count = length // SHORT
    blocks = signal.reshape(chan_width, block_count, SHORT)
    padded = jnp.concatenate([blocks, jnp.zeros_like(blocks)], axis=2)
    lagged = jnp.concatenate([jnp.zeros((chan_width, SHORT), jnp.float32), kernel], axis=1).reshape(
        chan_width, block_count + 1, SHORT
    )
    windows = jnp.concatenate([lagged[:, :-1], lagged[:, 1:]], axis=2)
    sig_real, sig_imag = forward_dft(padded)
    fil_real, fil_imag = forward_dft(windows)
    empty_freq = jnp.zeros_like(sig_real)
    pad_real = jnp.concatenate([empty_freq, sig_real], axis=1)
    pad_imag = jnp.concatenate([empty_freq, sig_imag], axis=1)

    def accumulate(shift_step, totals):
        keep_flag = jnp.where(shift_step == 0, 1.0, long_flag)
        moved_real = lax.dynamic_slice_in_dim(
            pad_real, block_count - shift_step, block_count, axis=1
        )
        moved_imag = lax.dynamic_slice_in_dim(
            pad_imag, block_count - shift_step, block_count, axis=1
        )
        part_real = lax.dynamic_slice_in_dim(fil_real, shift_step, 1, axis=1) * keep_flag
        part_imag = lax.dynamic_slice_in_dim(fil_imag, shift_step, 1, axis=1) * keep_flag
        return (
            totals[0] + moved_real * part_real - moved_imag * part_imag,
            totals[1] + moved_real * part_imag + moved_imag * part_real,
        )

    total_real, total_imag = lax.fori_loop(0, block_count, accumulate, (empty_freq, empty_freq))
    result = inverse_dft(total_real, total_imag)
    return result[:, :, SHORT:].reshape(chan_width, length)


def short_mix(projected, tap_weights, doc_pos):
    summed = tap_weights[0][:, :, None] * projected
    for lag_count in (1, 2):
        shifted = jnp.concatenate(
            [
                jnp.zeros(projected.shape[:2] + (lag_count,), jnp.float32),
                projected[:, :, :-lag_count],
            ],
            axis=2,
        )
        summed = (
            summed
            + tap_weights[lag_count][:, :, None]
            * shifted
            * (doc_pos >= lag_count).astype(jnp.float32)[None, None, :]
        )
    return summed


def mixer(
    projected, raw_filter, tap_weights, conv_shift, kind_here, stop_here, span_here, decay_rates
):
    length = projected.shape[2]
    offsets = jnp.arange(length, dtype=jnp.int32)
    doc_pos = jnp.where(kind_here == 1, offsets, offsets % SHORT)
    shorted = short_mix(projected, tap_weights, doc_pos)
    signal = shorted[0] * shorted[2]
    damping = jnp.exp(
        -offsets.astype(jnp.float32)[None, :] * decay_rates[:, None] / span_here.astype(jnp.float32)
    )
    inside = (offsets < stop_here).astype(jnp.float32)[None, :]
    kernel = raw_filter * damping * inside
    mixed_out = (
        blocked_conv(signal, kernel, kind_here.astype(jnp.float32)) + conv_shift[:, None] * signal
    )
    return shorted[1] * mixed_out


def local(
    tokens_in,
    ln_gain,
    ln_bias,
    in_weight,
    short_weight,
    filter_first,
    filter_mid,
    filter_last,
    conv_bias,
    out_weight,
    up_weight,
    down_weight,
    group_kind,
    filt_len,
    decay_win,
    cotangent,
):
    chan_count = lax.axis_size("chan")
    seq_count = lax.axis_size("seq")
    seq_index = lax.axis_index("seq")
    chan_index = lax.axis_index("chan")
    local_rows, width = tokens_in.shape
    group_len = local_rows * chan_count // 2
    spread = group_len // seq_count
    chan_width = conv_bias.shape[1]
    kinds = lax.dynamic_slice_in_dim(group_kind, 2 * seq_index, 2)
    stops = lax.dynamic_slice_in_dim(filt_len, 2 * seq_index, 2)
    spans = lax.dynamic_slice_in_dim(decay_win, 2 * seq_index, 2)
    global_chan = (chan_index * chan_width + jnp.arange(chan_width, dtype=jnp.int32)).astype(
        jnp.float32
    )
    decay_rates = jnp.exp(jnp.log(0.3) + jnp.log(100.0) * global_chan / (width - 1))
    positions = (seq_index * spread + jnp.arange(spread, dtype=jnp.int32)).astype(jnp.float32)
    features = position_features(positions, group_len)

    def mix_groups(proj_all, raw_all, taps, shift_all):

        def one_group(proj_one, kind_one, stop_one, span_one):
            return mixer(
                proj_one, raw_all, taps, shift_all, kind_one, stop_one, span_one, decay_rates
            )

        shaped = proj_all.reshape(3, chan_width, 2, group_len)
        mixed = jax.vmap(one_group, in_axes=(2, 0, 0, 0), out_axes=1)(shaped, kinds, stops, spans)
        return mixed.reshape(chan_width, 2 * group_len)

    stream = tokens_in
    kept_items = []
    for layer_index in range(LAYERS):
        gathered = (
            lax.all_gather(in_weight[layer_index], "chan", axis=0, tiled=True),
            lax.all_gather(out_weight[layer_index], "chan", axis=0, tiled=True),
            lax.all_gather(up_weight[layer_index], "chan", axis=0, tiled=True),
            lax.all_gather(down_weight[layer_index], "chan", axis=0, tiled=True),
            lax.all_gather(ln_gain[layer_index], "chan", axis=1, tiled=True),
            lax.all_gather(ln_bias[layer_index], "chan", axis=1, tiled=True),
        )
        w_in, w_out, w_up, w_down, gain_rows, shift_rows = gathered
        gain_rows = gain_rows.astype(jnp.float32)
        shift_rows = shift_rows.astype(jnp.float32)
        first_norm, first_back = jax.vjp(layer_norm, stream, gain_rows[0], shift_rows[0])
        normed_in = first_norm.astype(jnp.bfloat16)
        proj_cols = dot_cross(w_in, normed_in).astype(jnp.bfloat16).reshape(3, width, local_rows)
        by_channel = lax.all_to_all(proj_cols, "chan", split_axis=1, concat_axis=2, tiled=True)
        raw_local, filter_back = jax.vjp(
            lambda a, b, c: filter_columns(features, a, b, c),
            filter_first[layer_index],
            filter_mid[layer_index],
            filter_last[layer_index],
        )
        raw_whole = lax.all_gather(
            raw_local.astype(jnp.bfloat16), "seq", axis=1, tiled=True
        ).astype(jnp.float32)
        mixed_out, mixer_back = jax.vjp(
            mix_groups,
            by_channel.astype(jnp.float32),
            raw_whole,
            short_weight[layer_index],
            conv_bias[layer_index],
        )
        by_token = lax.all_to_all(
            mixed_out.astype(jnp.bfloat16), "chan", split_axis=1, concat_axis=0, tiled=True
        )
        middle_stream = stream + dot_lead(by_token, w_out)
        second_norm, second_back = jax.vjp(layer_norm, middle_stream, gain_rows[1], shift_rows[1])
        normed_mid = second_norm.astype(jnp.bfloat16)
        pre_act = jnp.dot(normed_mid, w_up, preferred_element_type=jnp.float32)
        hidden = jax.nn.gelu(pre_act, approximate=False).astype(jnp.bfloat16)
        stream = middle_stream + jnp.dot(hidden, w_down, preferred_element_type=jnp.float32)
        held_weights = None
        kept_items.append(
            (
                held_weights,
                first_back,
                normed_in,
                filter_back,
                mixer_back,
                by_token,
                second_back,
                normed_mid,
                pre_act,
                hidden,
            )
        )
    grad_stream = cotangent
    layer_grads = [None] * LAYERS
    local_grads = [None] * LAYERS
    for layer_index in reversed(range(LAYERS)):
        (
            held_weights,
            first_back,
            normed_in,
            filter_back,
            mixer_back,
            by_token,
            second_back,
            normed_mid,
            pre_act,
            hidden,
        ) = kept_items[layer_index]
        w_in, w_out, w_up, w_down = (
            lax.all_gather(in_weight[layer_index], "chan", axis=0, tiled=True),
            lax.all_gather(out_weight[layer_index], "chan", axis=0, tiled=True),
            lax.all_gather(up_weight[layer_index], "chan", axis=0, tiled=True),
            lax.all_gather(down_weight[layer_index], "chan", axis=0, tiled=True),
        )
        down_grad = grad_stream.astype(jnp.bfloat16)
        grad_w_down = dot_lead(hidden, down_grad)
        grad_hidden = dot_trail(down_grad, w_down)
        slope_grad = jax.vjp(lambda a: jax.nn.gelu(a, approximate=False), pre_act)[1](grad_hidden)[
            0
        ]
        up_grad = slope_grad.astype(jnp.bfloat16)
        grad_w_up = dot_lead(normed_mid, up_grad)
        grad_normed = dot_trail(up_grad, w_up)
        grad_mid, grad_gain_two, grad_shift_two = second_back(grad_normed)
        grad_mid = grad_stream + grad_mid
        out_grad = grad_mid.astype(jnp.bfloat16)
        grad_w_out = jnp.dot(by_token, out_grad, preferred_element_type=jnp.float32)
        grad_gated = dot_trail(w_out, out_grad).astype(jnp.bfloat16)
        grad_channel = lax.all_to_all(
            grad_gated, "chan", split_axis=0, concat_axis=1, tiled=True
        ).astype(jnp.float32)
        grad_proj, grad_raw, grad_taps, grad_cshift = mixer_back(grad_channel)
        proj_grad = lax.all_to_all(
            grad_proj.astype(jnp.bfloat16), "chan", split_axis=2, concat_axis=1, tiled=True
        ).reshape(3 * width, local_rows)
        grad_w_in = dot_cross(normed_in, proj_grad)
        grad_normed_in = dot_cross(proj_grad, w_in)
        grad_input, grad_gain_one, grad_shift_one = first_back(grad_normed_in)
        grad_stream = grad_mid + grad_input
        raw_grad = lax.psum_scatter(
            grad_raw.astype(jnp.bfloat16), "seq", scatter_dimension=1, tiled=True
        ).astype(jnp.float32)
        grad_first, grad_middle, grad_last = filter_back(raw_grad)
        gain_pair = jnp.stack([grad_gain_one, grad_gain_two])
        shift_pair = jnp.stack([grad_shift_one, grad_shift_two])
        layer_grads[layer_index] = (
            lax.psum_scatter(grad_w_in, "chan", scatter_dimension=0, tiled=True),
            lax.psum_scatter(grad_w_out, "chan", scatter_dimension=0, tiled=True),
            lax.psum_scatter(grad_w_up, "chan", scatter_dimension=0, tiled=True),
            lax.psum_scatter(grad_w_down, "chan", scatter_dimension=0, tiled=True),
            lax.psum_scatter(gain_pair, "chan", scatter_dimension=1, tiled=True),
            lax.psum_scatter(shift_pair, "chan", scatter_dimension=1, tiled=True),
        )
        local_grads[layer_index] = (grad_taps, grad_cshift, grad_last, grad_first, grad_middle)
    stack_in = jnp.stack([layer_grads[i][0] for i in range(LAYERS)])
    stack_out = jnp.stack([layer_grads[i][1] for i in range(LAYERS)])
    stack_up = jnp.stack([layer_grads[i][2] for i in range(LAYERS)])
    stack_down = jnp.stack([layer_grads[i][3] for i in range(LAYERS)])
    stack_gain = jnp.stack([layer_grads[i][4] for i in range(LAYERS)])
    stack_shift = jnp.stack([layer_grads[i][5] for i in range(LAYERS)])
    taps_all = jnp.stack([local_grads[i][0] for i in range(LAYERS)])
    cshift_all = jnp.stack([local_grads[i][1] for i in range(LAYERS)])
    last_all = jnp.stack([local_grads[i][2] for i in range(LAYERS)])
    first_all = jnp.stack([local_grads[i][3] for i in range(LAYERS)])
    middle_all = jnp.stack([local_grads[i][4] for i in range(LAYERS)])
    summed = (
        lax.psum(stack_in.astype(jnp.bfloat16), "seq").astype(jnp.float32),
        lax.psum(stack_out.astype(jnp.bfloat16), "seq").astype(jnp.float32),
        lax.psum(stack_up.astype(jnp.bfloat16), "seq").astype(jnp.float32),
        lax.psum(stack_down.astype(jnp.bfloat16), "seq").astype(jnp.float32),
        lax.psum(stack_gain.astype(jnp.bfloat16), "seq").astype(jnp.float32),
        lax.psum(stack_shift.astype(jnp.bfloat16), "seq").astype(jnp.float32),
        lax.psum(taps_all.astype(jnp.bfloat16), "seq").astype(jnp.float32),
        lax.psum(cshift_all.astype(jnp.bfloat16), "seq").astype(jnp.float32),
        lax.psum(last_all.astype(jnp.bfloat16), "seq").astype(jnp.float32),
    )
    core_sums = lax.psum((first_all, middle_all), ("seq", "chan"))
    return (
        stream,
        grad_stream,
        summed[4],
        summed[5],
        summed[0],
        summed[6],
        core_sums[0],
        core_sums[1],
        summed[8],
        summed[7],
        summed[1],
        summed[2],
        summed[3],
    )


def transform_tables():
    freq = np.concatenate([np.arange(0, HALF, 2), np.arange(1, HALF, 2)])
    tables = []
    for parity in range(2):
        time = 2 * np.arange(HALF) + parity
        turns = ((2 * freq[:, None] + 1) * time[None, :]) % (4 * BLOCK)
        angles = turns * (np.pi / (2 * BLOCK))
        tables.append(np.concatenate([np.cos(angles), -np.sin(angles)]))
    table = np.stack(tables).astype(ml_dtypes.bfloat16)
    return table, np.ascontiguousarray(table.transpose(0, 2, 1))


def matmul(left, right):
    return jnp.dot(left, right, preferred_element_type=F32)


def row_slices():
    return [pl.ds(k * HALF, HALF) for k in range(4)]


def to_spectrum(dft_ref, even, odd, store):
    even, odd = matmul(dft_ref[0], even), matmul(dft_ref[1], odd)
    store(0, even[:HALF] + odd[:HALF])
    store(1, even[:HALF] - odd[:HALF])
    store(2, even[HALF:] + odd[HALF:])
    store(3, odd[HALF:] - even[HALF:])


def from_spectrum(inverse_ref, parts):
    scale = 1.0 / BLOCK
    even = jnp.concatenate([(parts[0] + parts[1]).astype(BF16), (parts[2] - parts[3]).astype(BF16)], axis=0)
    odd = jnp.concatenate([(parts[0] - parts[1]).astype(BF16), (parts[2] + parts[3]).astype(BF16)], axis=0)
    return matmul(inverse_ref[0], even) * scale, matmul(inverse_ref[1], odd) * scale


def block_offsets(block):
    row = lax.broadcasted_iota(jnp.int32, (BLOCK, TILE), 0)
    return block * BLOCK + jnp.where(row < HALF, 2 * row, 2 * (row - HALF) + 1)


def window_kernel(place_ref, hidden_ref, last_ref, rate_ref, dft_ref, out_ref, before, table):
    d = pl.program_id(1)
    slowness = rate_ref[...] / place_ref[4].astype(F32)

    @pl.when(d == 0)
    def _():
        before[...] = jnp.zeros_like(before)
        table[...] = jnp.exp(-block_offsets(0).astype(F32) * slowness)

    @pl.when(d <= 2 * jnp.maximum(place_ref[0], place_ref[1]) + 1)
    def _():
        raw = matmul(hidden_ref[...], last_ref[...]).astype(BF16).astype(F32)
        fade = jnp.exp(-(d * BLOCK).astype(F32) * slowness)
        taps = jnp.where(block_offsets(d) < place_ref[3], raw * (table[...] * fade), 0.0).astype(BF16)
        slices = row_slices()
        now = [None] * 4

        def keep(k, rows):
            now[k] = rows

        to_spectrum(dft_ref, taps[:HALF], taps[HALF:], keep)
        sign = jnp.where(lax.broadcasted_iota(jnp.int32, (HALF, TILE), 0) < HALF // 2, 1.0, -1.0)
        out_ref[0, slices[0], :] = (now[0] - sign * before[slices[2], :]).astype(BF16)
        out_ref[0, slices[1], :] = (now[1] + sign * before[slices[3], :]).astype(BF16)
        out_ref[0, slices[2], :] = (now[2] + sign * before[slices[0], :]).astype(BF16)
        out_ref[0, slices[3], :] = (now[3] - sign * before[slices[1], :]).astype(BF16)
        for k in range(4):
            before[slices[k], :] = now[k]


def window_spectra(place, hidden, last, rates, dft):
    length, inner = hidden.shape
    width = last.shape[1]
    count = length // BLOCK
    return pl.pallas_call(
        window_kernel,
        grid_spec=pltpu.PrefetchScalarGridSpec(
            num_scalar_prefetch=1,
            grid=(width // TILE, count),
            in_specs=[
                pl.BlockSpec((BLOCK, inner), lambda c, d, *_: (d, 0)),
                pl.BlockSpec((inner, TILE), lambda c, d, *_: (0, c)),
                pl.BlockSpec((1, TILE), lambda c, d, *_: (0, c)),
                pl.BlockSpec(dft.shape, lambda c, d, *_: (0, 0, 0)),
            ],
            out_specs=pl.BlockSpec((1, 2 * BLOCK, TILE), lambda c, d, *_: (d, 0, c)),
            scratch_shapes=[pltpu.VMEM((2 * BLOCK, TILE), F32), pltpu.VMEM((BLOCK, TILE), F32)],
        ),
        out_shape=jax.ShapeDtypeStruct((count, 2 * BLOCK, width), BF16),
        compiler_params=pltpu.CompilerParams(vmem_limit_bytes=32 * MIB),
        cost_estimate=LIGHT,
        name="window_spectra",
    )(place, hidden, last, rates, dft)


ROWS_STEP = 16


def load_pair(ref, block, base):
    real = ref[block, pl.ds(base, ROWS_STEP), :].astype(F32)
    imag = ref[block, pl.ds(BLOCK + base, ROWS_STEP), :].astype(F32)
    return real, imag


def add_pair(ref, block, base, real, imag):
    ref[block, pl.ds(base, ROWS_STEP), :] += real
    ref[block, pl.ds(BLOCK + base, ROWS_STEP), :] += imag


def product(a, b):
    return a[0] * b[0] - a[1] * b[1], a[0] * b[1] + a[1] * b[0]


def conj_product(a, b):
    return a[0] * b[0] + a[1] * b[1], a[0] * b[1] - a[1] * b[0]


def plus(a, b):
    return a[0] + b[0], a[1] + b[1]


def interleave(woven, block, parity, rows):
    for side in range(TILE // 128):
        at = pl.ds(block * BLOCK + parity, HALF, stride=2)
        woven[side, at, :] = rows[:, side * 128 : side * 128 + 128]


def transform_blocks(dft_ref, target, source):
    for b in range(2):
        slices = row_slices()

        def store(k, rows, b=b, slices=slices):
            target[b, slices[k], :] = rows

        to_spectrum(
            dft_ref, source[pl.ds(b * BLOCK, HALF), :], source[pl.ds(b * BLOCK + HALF, HALF), :], store
        )


def over_rows(body):
    def one(index, carry):
        body(pl.multiple_of(index * ROWS_STEP, ROWS_STEP))
        return carry

    lax.fori_loop(0, BLOCK // ROWS_STEP, one, 0, unroll=8)


def each_hop(place_ref, later, body):
    hops = place_ref[1] if later else place_ref[0]
    near = place_ref[2] == (0 if later else 1)
    pl.when((hops >= 1) & near)(lambda: body(1, 1))
    pl.when((hops >= 1) & jnp.logical_not(near))(lambda: body(1, 3))
    pl.when(hops >= 2)(lambda: body(2, 2))
    pl.when(hops >= 3)(lambda: body(3, 3))


def conv_forward_kernel(
    place_ref, own, partner, far, beyond, window_ref, dft_ref, inverse_ref, gate_ref, shift_ref,
    gated_ref, conv_ref, spec, total, woven,
):
    sources = (own, partner, far, beyond)

    def transform(source):
        transform_blocks(dft_ref, spec, source)

    def gather(hop, which):
        transform(sources[which])
        lag = 2 * hop

        def body(base):
            first, second = load_pair(spec, 0, base), load_pair(spec, 1, base)
            here, after = load_pair(window_ref, lag, base), load_pair(window_ref, lag + 1, base)
            one = product(first, here)
            two = plus(product(first, after), product(second, here))
            if hop == 0:
                for block, value in ((0, one), (1, two)):
                    total[block, pl.ds(base, ROWS_STEP), :] = value[0]
                    total[block, pl.ds(BLOCK + base, ROWS_STEP), :] = value[1]
            else:
                one = plus(one, product(second, load_pair(window_ref, lag - 1, base)))
                add_pair(total, 0, base, *one)
                add_pair(total, 1, base, *two)

        over_rows(body)

    gather(0, 0)
    each_hop(place_ref, False, gather)
    for b in range(2):
        parts = from_spectrum(inverse_ref, [total[b, rows, :] for rows in row_slices()])
        for parity, result in enumerate(parts):
            held = own[pl.ds(b * BLOCK + parity * HALF, HALF), :].astype(F32)
            interleave(woven, b, parity, result + shift_ref[...] * held)
    for side in range(TILE // 128):
        lanes = pl.ds(side * 128, 128)
        conv_ref[:, lanes] = woven[side].astype(BF16)
        gated_ref[:, lanes] = (woven[side] * gate_ref[:, lanes].astype(F32)).astype(BF16)


def conv_forward(place, own, partner, far, beyond, windows, dft, inverse, gate, shift):
    rows, width = own.shape
    tile = pl.BlockSpec((rows, TILE), lambda c, *_: (0, c))
    return pl.pallas_call(
        conv_forward_kernel,
        grid_spec=pltpu.PrefetchScalarGridSpec(
            num_scalar_prefetch=1,
            grid=(width // TILE,),
            in_specs=[tile] * 4
            + [
                pl.BlockSpec((windows.shape[0], 2 * BLOCK, TILE), lambda c, *_: (0, 0, c)),
                pl.BlockSpec(dft.shape, lambda c, *_: (0, 0, 0)),
                pl.BlockSpec(inverse.shape, lambda c, *_: (0, 0, 0)),
                tile,
                pl.BlockSpec((1, TILE), lambda c, *_: (0, c)),
            ],
            out_specs=[tile] * 2,
            scratch_shapes=[
                pltpu.VMEM((2, 2 * BLOCK, TILE), F32),
                pltpu.VMEM((2, 2 * BLOCK, TILE), F32),
                pltpu.VMEM((TILE // 128, rows, 128), F32),
            ],
        ),
        out_shape=[jax.ShapeDtypeStruct((rows, width), BF16)] * 2,
        compiler_params=pltpu.CompilerParams(vmem_limit_bytes=48 * MIB),
        cost_estimate=LIGHT,
        name="conv_forward",
    )(place, own, partner, far, beyond, windows, dft, inverse, gate, shift)


def conv_backward_kernel(
    place_ref, own, partner, far, beyond, g_own, g_partner, g_far, g_beyond, window_ref, dft_ref, inverse_ref,
    first, second, third, edge_one, edge_two, edge_three, taps_ref, shift_ref, g_gated_ref, conv_ref, rate_ref,
    hidden_ref, last_ref, g_proj_ref, g_edge_ref, g_last_ref, g_middle_ref, g_taps_ref, g_shift_ref,
    g_spec, spec, g_total, g_window, spread, woven,
):
    rows = own.shape[0]
    count = g_window.shape[0] - 1

    def transform(target, source):
        transform_blocks(dft_ref, target, source)

    g_sources = (g_own, g_partner, g_far, g_beyond)
    sources = (own, partner, far, beyond)
    g_total[...] = jnp.zeros_like(g_total)
    g_window[...] = jnp.zeros_like(g_window)

    def pull(hop, which):
        lag = 2 * hop
        held = g_spec
        if hop > 0:
            transform(spec, g_sources[which])
            held = spec

        def body(base):
            one, two = load_pair(held, 0, base), load_pair(held, 1, base)
            here, after = load_pair(window_ref, lag, base), load_pair(window_ref, lag + 1, base)
            add_pair(g_total, 0, base, *plus(conj_product(here, one), conj_product(after, two)))
            other = conj_product(here, two)
            if hop > 0:
                other = plus(other, conj_product(load_pair(window_ref, lag - 1, base), one))
            add_pair(g_total, 1, base, *other)

        over_rows(body)

    def push(hop, which):
        lag = 2 * hop
        transform(spec, sources[which])

        def body(base):
            x_one, x_two = load_pair(spec, 0, base), load_pair(spec, 1, base)
            one, two = load_pair(g_spec, 0, base), load_pair(g_spec, 1, base)
            add_pair(g_window, lag, base, *plus(conj_product(x_one, one), conj_product(x_two, two)))
            add_pair(g_window, lag + 1, base, *conj_product(x_one, two))
            if hop > 0:
                add_pair(g_window, lag - 1, base, *conj_product(x_two, one))

        over_rows(body)

    transform(g_spec, g_own)
    pull(0, 0)
    each_hop(place_ref, True, pull)
    push(0, 0)
    each_hop(place_ref, False, push)

    stop = place_ref[3]
    slowness = rate_ref[...] / place_ref[4].astype(F32)
    last_bf = last_ref[...].astype(BF16)
    table = spec.at[1, pl.ds(0, BLOCK)]
    table[...] = jnp.exp(-block_offsets(0).astype(F32) * slowness)
    g_last_ref[...] = jnp.zeros_like(g_last_ref)

    @pl.when(pl.program_id(0) == 0)
    def _():
        g_middle_ref[...] = jnp.zeros_like(g_middle_ref)

    for d in range(count):
        @pl.when(d <= 2 * place_ref[0] + 1)
        def _():
            slices = row_slices()
            sign = jnp.where(lax.broadcasted_iota(jnp.int32, (HALF, TILE), 0) < HALF // 2, 1.0, -1.0)
            here = [g_window[d, rows, :] for rows in slices]
            after = [g_window[d + 1, rows, :] for rows in slices]
            parts = [
                here[0] + sign * after[2], here[1] - sign * after[3],
                here[2] - sign * after[0], here[3] + sign * after[1],
            ]
            lags = jnp.concatenate(from_spectrum(inverse_ref, parts), axis=0)
            fade = jnp.exp(-float(d * BLOCK) * slowness)
            g_raw = jnp.where(block_offsets(d) < stop, lags * (table[...] * fade), 0.0).astype(BF16)
            at = pl.ds(d * BLOCK, BLOCK)
            g_last_ref[...] += matmul(hidden_ref[:, at], g_raw)
            g_middle_ref[at, :] += lax.dot_general(
                g_raw, last_bf, (((1,), (1,)), ((), ())), preferred_element_type=F32
            )

    for b in range(2):
        parts = from_spectrum(inverse_ref, [g_total[b, rows, :] for rows in row_slices()])
        for parity, result in enumerate(parts):
            held = g_own[pl.ds(b * BLOCK + parity * HALF, HALF), :].astype(F32)
            interleave(woven, b, parity, result + shift_ref[...] * held)

    for k, (source, edge) in enumerate(((first, edge_one), (second, edge_two), (third, edge_three))):
        spread[k, pl.ds(0, EDGE), :] = edge[0].astype(F32)
        spread[k, pl.ds(EDGE, rows), :] = source[...].astype(F32)
    step = 32
    g_taps_ref[...] = jnp.zeros_like(g_taps_ref)
    g_shift_ref[...] = jnp.zeros_like(g_shift_ref)

    def fold(values):
        return jnp.sum(values.reshape(step // 8, 8, TILE), axis=0)

    def shifts(k, base):
        window = spread[k, pl.ds(pl.multiple_of(base + EDGE - 8, 8), step + 8), :]
        return [window[8:]] + [pltpu.roll(window, lag, 0)[8:] for lag in (1, 2)]

    def tapped(k, parts):
        total = taps_ref[k : k + 1, :] * parts[0]
        for lag in (1, 2):
            total = total + taps_ref[3 * lag + k : 3 * lag + k + 1, :] * parts[lag]
        return total

    def one(index, carry):
        base = pl.multiple_of(index * step, step)
        at = pl.ds(base, step)
        g_signal = jnp.concatenate([woven[side, at, :] for side in range(TILE // 128)], axis=1)
        g_shift_ref[...] += fold(g_own[at, :].astype(F32) * own[at, :].astype(F32))
        parts = shifts(0, base)
        g_third = g_signal * tapped(0, parts)
        more = shifts(2, base)
        g_first = g_signal * tapped(2, more)
        for lag in range(3):
            g_taps_ref[3 * lag] += fold(g_first * parts[lag])
            g_taps_ref[3 * lag + 2] += fold(g_third * more[lag])
        g_window[0, at, :] = g_first
        g_window[2, at, :] = g_third
        g_second = g_gated_ref[at, :].astype(F32) * conv_ref[at, :].astype(F32)
        parts = shifts(1, base)
        for lag in range(3):
            g_taps_ref[3 * lag + 1] += fold(g_second * parts[lag])
        g_window[1, at, :] = g_second
        return carry

    lax.fori_loop(0, rows // step, one, 0, unroll=4)

    for k in range(3):
        g_edge_ref[k] = g_window[k, pl.ds(0, EDGE), :].astype(BF16)

    def two(index, carry):
        base = pl.multiple_of(index * step, step)
        at = pl.ds(base, step)
        for k in range(3):
            window = spread[k, pl.ds(base, step + 8), :]
            total = taps_ref[k : k + 1, :] * window[:step]
            for lag in (1, 2):
                moved = pltpu.roll(window, step + 8 - lag, 0)[:step]
                total = total + taps_ref[3 * lag + k : 3 * lag + k + 1, :] * moved
            g_proj_ref[k, at, :] = total.astype(BF16)
        return carry

    for k in range(3):
        spread[k, pl.ds(0, rows), :] = g_window[k, pl.ds(0, rows), :]
        spread[k, pl.ds(rows, EDGE), :] = jnp.zeros((EDGE, TILE), F32)
    lax.fori_loop(0, rows // step, two, 0, unroll=4)


def conv_backward(
    place, signals, g_convs, windows, dft, inverse, projected, edge, taps, shift, g_gated, conv, rates, hidden, last
):
    rows, width = g_gated.shape
    count = windows.shape[0]
    tiles = width // TILE
    tile = pl.BlockSpec((rows, TILE), lambda c, *_: (0, c))
    line = pl.BlockSpec((1, TILE), lambda c, *_: (0, c))

    def edge_at(k):
        return lambda c, *_: (k, 0, c)

    return pl.pallas_call(
        conv_backward_kernel,
        grid_spec=pltpu.PrefetchScalarGridSpec(
            num_scalar_prefetch=1,
            grid=(tiles,),
            in_specs=[tile] * 8
            + [
                pl.BlockSpec((count, 2 * BLOCK, TILE), lambda c, *_: (0, 0, c)),
                pl.BlockSpec(dft.shape, lambda c, *_: (0, 0, 0)),
                pl.BlockSpec(inverse.shape, lambda c, *_: (0, 0, 0)),
            ]
            + [tile] * 3
            + [pl.BlockSpec((1, EDGE, TILE), edge_at(k)) for k in range(3)]
            + [
                pl.BlockSpec((9, TILE), lambda c, *_: (0, c)), line, tile, tile, line,
                pl.BlockSpec(hidden.shape, lambda c, *_: (0, 0)),
                pl.BlockSpec((hidden.shape[0], TILE), lambda c, *_: (0, c)),
            ],
            out_specs=[
                pl.BlockSpec((3, rows, TILE), lambda c, *_: (0, 0, c)),
                pl.BlockSpec((3, EDGE, TILE), lambda c, *_: (0, 0, c)),
                pl.BlockSpec((hidden.shape[0], TILE), lambda c, *_: (0, c)),
                pl.BlockSpec((count * BLOCK, hidden.shape[0]), lambda c, *_: (0, 0)),
                pl.BlockSpec((9, 8, TILE), lambda c, *_: (0, 0, c)),
                pl.BlockSpec((8, TILE), lambda c, *_: (0, c)),
            ],
            scratch_shapes=[
                pltpu.VMEM((2, 2 * BLOCK, TILE), F32),
                pltpu.VMEM((2, 2 * BLOCK, TILE), F32),
                pltpu.VMEM((2, 2 * BLOCK, TILE), F32),
                pltpu.VMEM((count + 1, 2 * BLOCK, TILE), F32),
                pltpu.VMEM((3, rows + EDGE, TILE), F32),
                pltpu.VMEM((TILE // 128, rows, 128), F32),
            ],
        ),
        out_shape=[
            jax.ShapeDtypeStruct((3, rows, width), BF16),
            jax.ShapeDtypeStruct((3, EDGE, width), BF16),
            jax.ShapeDtypeStruct((hidden.shape[0], width), F32),
            jax.ShapeDtypeStruct((count * BLOCK, hidden.shape[0]), F32),
            jax.ShapeDtypeStruct((9, 8, width), F32),
            jax.ShapeDtypeStruct((8, width), F32),
        ],
        compiler_params=pltpu.CompilerParams(vmem_limit_bytes=60 * MIB),
        cost_estimate=LIGHT,
        name="conv_backward",
    )(
        place, *signals, *g_convs, windows, dft, inverse, *projected,
        edge, edge, edge, taps, shift, g_gated, conv, rates, hidden, last,
    )


PIECES = 2
NEAR = (((1,), (1,)), ((), ()))
LEAD = (((0,), (0,)), ((), ()))


def matmul_near(left, right):
    return lax.dot_general(left, right, NEAR, preferred_element_type=F32)


def matmul_lead(left, right):
    return lax.dot_general(left, right, LEAD, preferred_element_type=F32)


def strip_of(z, c):
    return pl.multiple_of((2 * z + c) * STRIP, STRIP)


def start_columns(place_ref, pieces, which, target, sem, part):
    z, c = place_ref[6], place_ref[7]
    for dc in range(2):
        own, others = pieces[dc * PIECES], pieces[dc * PIECES + 1]
        to = target.at[pl.ds(strip_of(z, c ^ dc), STRIP), :]
        pltpu.make_async_copy(own.at[part, which], to, sem).start()
        for dz in range(1, 4):
            to = target.at[pl.ds(strip_of(z ^ dz, c ^ dc), STRIP), :]
            pltpu.make_async_copy(others.at[part, dz - 1, which], to, sem).start()


def start_rows(place_ref, pieces, which, target, sem, line):
    z, c = place_ref[6], place_ref[7]
    dz = z ^ line
    for dc in range(2):
        own, others = pieces[dc * PIECES], pieces[dc * PIECES + 1]
        for part in range(4):
            row = pl.multiple_of((c ^ dc) * 4 * STRIP + part * STRIP, STRIP)
            to = target.at[pl.ds(row, STRIP), :]

            @pl.when(dz == 0)
            def _():
                pltpu.make_async_copy(own.at[part, which], to, sem).start()

            @pl.when(dz > 0)
            def _():
                pltpu.make_async_copy(others.at[part, jnp.maximum(dz - 1, 0), which], to, sem).start()


def wait_whole(target, sem):
    pltpu.make_async_copy(target, target, sem).wait()


def norm_rows(values, gain, bias):
    average = jnp.mean(values, axis=-1, keepdims=True)
    centred = values - average
    variance = jnp.mean(centred * centred, axis=-1, keepdims=True)
    return centred * lax.rsqrt(variance + 1e-05) * gain + bias


def loop_rows(count, step, body, unroll=1):
    def one(index, carry):
        body(pl.multiple_of(index * step, step))
        return carry

    lax.fori_loop(0, count // step, one, 0, unroll=unroll)


def part_rows(woven, first, target):
    for side in range(woven.shape[0]):
        for block in range(0, woven.shape[1], BLOCK):
            for parity in range(2):
                rows = woven[side, pl.ds(block + parity, HALF, stride=2), :]
                at = pl.ds(first + block + parity * HALF, HALF)
                target[at, pl.ds(side * 128, 128)] = rows.astype(BF16)


def project_kernel(place_ref, stream, above, gain, bias, taps_ref, *rest):
    pieces = rest[: 2 * PIECES]
    normed_ref, one_ref, two_ref, three_ref, edge_ref, signal_ref, gate_ref, weights, held, spread, product_held, sem = rest[2 * PIECES :]
    rows = stream.shape[0]
    step_index = pl.program_id(0)

    @pl.when(step_index == 0)
    def _():
        for part in range(3):
            start_columns(place_ref, pieces, 0, weights.at[part], sem, part)

        head = norm_rows(above[...], gain[...], bias[...])
        held[pl.ds(0, EDGE), :] = jnp.where(place_ref[0] > 0, head, 0.0).astype(BF16)

        def body(base):
            values = norm_rows(stream[pl.ds(base, 128), :], gain[...], bias[...]).astype(BF16)
            held[pl.ds(pl.multiple_of(EDGE + base, EDGE), 128), :] = values
            normed_ref[pl.ds(base, 128), :] = values

        loop_rows(rows, 128, body)
        wait_whole(weights, sem)

    tile_at = pl.ds(pl.multiple_of(step_index * TILE, TILE), TILE)
    for k, ref in enumerate((one_ref, two_ref, three_ref)):
        result = matmul(held[...], weights[k, :, tile_at]).astype(BF16)
        ref[...] = result[EDGE:]
        edge_ref[k] = result[:EDGE]
        spread[k] = result.astype(F32)

    def body(base):
        mixed = []
        for k in range(3):
            window = spread[k, pl.ds(pl.multiple_of(base + EDGE - 8, 8), 40), :]
            total = taps_ref[k : k + 1, :] * window[8:]
            for lag in (1, 2):
                moved = pltpu.roll(window, lag, 0)[8:]
                total = total + taps_ref[3 * lag + k : 3 * lag + k + 1, :] * moved
            mixed.append(total)
        at = pl.ds(base, 32)
        signal = mixed[0] * mixed[2]
        for side in range(TILE // 128):
            product_held[side, at, :] = signal[:, side * 128 : side * 128 + 128]
        gate_ref[at, :] = mixed[1].astype(BF16)

    loop_rows(rows, 32, body, unroll=8)
    part_rows(product_held, 0, signal_ref)


def once(shape):
    zeros = (0,) * len(shape)
    return pl.BlockSpec(shape, lambda *_: zeros, pipeline_mode=pl.Buffered(1))


ANYWHERE = pl.BlockSpec(memory_space=pl.ANY)


def project(place, stream, above, gain, bias, taps, pieces):
    rows, width = stream.shape
    tile = pl.BlockSpec((rows, TILE), lambda c, *_: (0, c))
    return pl.pallas_call(
        project_kernel,
        grid_spec=pltpu.PrefetchScalarGridSpec(
            num_scalar_prefetch=1,
            grid=(width // TILE,),
            in_specs=[
                once((rows, width)), once((EDGE, width)), once((1, width)), once((1, width)),
                pl.BlockSpec((9, TILE), lambda c, *_: (0, c)),
            ]
            + [ANYWHERE] * (2 * PIECES),
            out_specs=[once((rows, width)), tile, tile, tile,
                       pl.BlockSpec((3, EDGE, TILE), lambda c, *_: (0, 0, c)), tile, tile],
            scratch_shapes=[
                pltpu.VMEM((3, width, width), BF16),
                pltpu.VMEM((rows + EDGE, width), BF16),
                pltpu.VMEM((3, rows + EDGE, TILE), F32),
                pltpu.VMEM((TILE // 128, rows, 128), F32),
                pltpu.SemaphoreType.DMA,
            ],
        ),
        out_shape=[jax.ShapeDtypeStruct((rows, width), BF16)] * 4
        + [jax.ShapeDtypeStruct((3, EDGE, width), BF16)]
        + [jax.ShapeDtypeStruct((rows, width), BF16)] * 2,
        compiler_params=pltpu.CompilerParams(vmem_limit_bytes=48 * MIB),
        cost_estimate=LIGHT,
        name="project",
    )(place, stream, above, gain, bias, taps, *pieces)


def gelu_and_slope(values):
    size = jnp.abs(values)
    bell = jnp.exp(-0.5 * values * values)
    t = pl.reciprocal(1.0 + (0.3275911 * math.sqrt(0.5)) * size)
    tail = 0.5 * 1.061405429 * t + 0.5 * -1.453152027
    tail = tail * t + 0.5 * 1.421413741
    tail = tail * t + 0.5 * -0.284496736
    tail = tail * t + 0.5 * 0.254829592
    tail = tail * t * bell
    below = jnp.where(values < 0.0, tail, 1.0 - tail)
    return values * below, below + values * bell * (1.0 / math.sqrt(2.0 * math.pi))


def feed_kernel(place_ref, stream, gated, gain, bias, *rest):
    mixer_pieces, feed_pieces = rest[: 2 * PIECES], rest[2 * PIECES : 4 * PIECES]
    (out_ref, middle_ref, normed_ref, hidden_ref, slope_ref, w_out, w_up, w_down,
     out_sem, up_sem, down_sem) = rest[4 * PIECES :]
    rows = stream.shape[0]
    step_index = pl.program_id(0)
    slot = step_index % 2

    def fetch(part):
        start_columns(place_ref, feed_pieces, 0, w_up.at[part % 2], up_sem.at[part % 2], part)
        start_rows(place_ref, feed_pieces, 1, w_down.at[part % 2], down_sem.at[part % 2], part)

    @pl.when(step_index == 0)
    def _():
        start_columns(place_ref, mixer_pieces, 0, w_out, out_sem, 3)
        fetch(0)
        wait_whole(w_out, out_sem)

        def body(base):
            at = pl.ds(base, 512)
            middle_ref[at, :] = stream[at, :] + matmul(gated[at, :], w_out[...])

        loop_rows(rows, 512, body)

        def norm(base):
            at = pl.ds(base, 128)
            middle = middle_ref[at, :]
            out_ref[at, :] = middle
            normed_ref[at, :] = norm_rows(middle, gain[...], bias[...]).astype(BF16)

        loop_rows(rows, 128, norm)

    for part in range(1, 4):
        @pl.when(step_index == part - 1)
        def _():
            fetch(part)

    wait_whole(w_up.at[slot], up_sem.at[slot])
    wait_whole(w_down.at[slot], down_sem.at[slot])

    def body(base):
        at = pl.ds(base, 512)
        pre_act = matmul(normed_ref[at, :], w_up[slot])
        hidden, slope = gelu_and_slope(pre_act)
        hidden = hidden.astype(BF16)
        hidden_ref[at, :] = hidden
        slope_ref[at, :] = slope.astype(BF16)
        out_ref[at, :] += matmul(hidden, w_down[slot])

    loop_rows(rows, 512, body)


def feed_forward(place, stream, gated, gain, bias, mixer_pieces, feed_pieces):
    rows, width = stream.shape
    part = pl.BlockSpec((rows, width), lambda j, *_: (0, j))
    return pl.pallas_call(
        feed_kernel,
        grid_spec=pltpu.PrefetchScalarGridSpec(
            num_scalar_prefetch=1,
            grid=(4,),
            in_specs=[once((rows, width)), once((rows, width)), once((1, width)), once((1, width))]
            + [ANYWHERE] * (4 * PIECES),
            out_specs=[once((rows, width)), once((rows, width)), once((rows, width)), part, part],
            scratch_shapes=[
                pltpu.VMEM((width, width), BF16),
                pltpu.VMEM((2, width, width), BF16),
                pltpu.VMEM((2, width, width), BF16),
                pltpu.SemaphoreType.DMA,
                pltpu.SemaphoreType.DMA((2,)),
                pltpu.SemaphoreType.DMA((2,)),
            ],
        ),
        out_shape=[
            jax.ShapeDtypeStruct((rows, width), F32),
            jax.ShapeDtypeStruct((rows, width), F32),
            jax.ShapeDtypeStruct((rows, width), BF16),
            jax.ShapeDtypeStruct((rows, 4 * width), BF16),
            jax.ShapeDtypeStruct((rows, 4 * width), BF16),
        ],
        compiler_params=pltpu.CompilerParams(vmem_limit_bytes=56 * MIB),
        cost_estimate=LIGHT,
        name="feed_forward",
    )(place, stream, gated, gain, bias, *mixer_pieces, *feed_pieces)


def norm_backward(values, g_normed, gain):
    average = jnp.mean(values, axis=-1, keepdims=True)
    centred = values - average
    variance = jnp.mean(centred * centred, axis=-1, keepdims=True)
    scale = lax.rsqrt(variance + 1e-05)
    unit = centred * scale
    g_unit = g_normed * gain
    inner = g_unit - jnp.mean(g_unit, axis=-1, keepdims=True)
    inner = inner - unit * jnp.mean(g_unit * unit, axis=-1, keepdims=True)
    return inner * scale, g_normed * unit


def fold_rows(values):
    return jnp.sum(values.reshape(values.shape[0] // 8, 8, values.shape[1]), axis=0)


def feed_backward_kernel(place_ref, g_stream, middle, gain, gate, slope_ref, *rest):
    mixer_pieces, feed_pieces = rest[: 2 * PIECES], rest[2 * PIECES : 4 * PIECES]
    (g_down_ref, g_pre_ref, g_mid_ref, g_out_ref, g_gated_ref, g_conv_ref, g_gain_ref, g_bias_ref,
     w_out, w_up, w_down, total, woven, out_sem, up_sem, down_sem) = rest[4 * PIECES :]
    rows = g_stream.shape[0]
    step_index = pl.program_id(0)
    slot = step_index % 2

    def fetch(part):
        start_columns(place_ref, feed_pieces, 0, w_up.at[part % 2], up_sem.at[part % 2], part)
        start_rows(place_ref, feed_pieces, 1, w_down.at[part % 2], down_sem.at[part % 2], part)

    @pl.when(step_index == 0)
    def _():
        fetch(0)
        start_columns(place_ref, mixer_pieces, 0, w_out, out_sem, 3)
        g_down_ref[...] = g_stream[...].astype(BF16)
        total[...] = jnp.zeros_like(total)

    for part in range(1, 4):
        @pl.when(step_index == part - 1)
        def _():
            fetch(part)

    wait_whole(w_up.at[slot], up_sem.at[slot])
    wait_whole(w_down.at[slot], down_sem.at[slot])

    def body(base):
        at = pl.ds(base, 512)
        g_hidden = matmul_near(g_down_ref[at, :], w_down[slot])
        g_pre = (g_hidden * slope_ref[at, :].astype(F32)).astype(BF16)
        g_pre_ref[at, :] = g_pre
        total[at, :] += matmul_near(g_pre, w_up[slot])

    loop_rows(rows, 512, body)

    @pl.when(step_index == 3)
    def _():
        wait_whole(w_out, out_sem)
        g_gain_ref[...] = jnp.zeros_like(g_gain_ref)
        g_bias_ref[...] = jnp.zeros_like(g_bias_ref)

        def last(base):
            at = pl.ds(base, 128)
            g_normed = total[at, :]
            g_value, g_scaled = norm_backward(middle[at, :], g_normed, gain[...])
            g_mid = g_stream[at, :] + g_value
            g_mid_ref[at, :] = g_mid
            g_out_ref[at, :] = g_mid.astype(BF16)
            g_gain_ref[...] += fold_rows(g_scaled)
            g_bias_ref[...] += fold_rows(g_normed)

        loop_rows(rows, 128, last)

        for first in range(0, rows, BLOCK):
            at = pl.ds(first, BLOCK)
            g_gated = matmul_near(g_out_ref[at, :], w_out[...]).astype(BF16)
            g_gated_ref[at, :] = g_gated
            g_conv = g_gated.astype(F32) * gate[at, :].astype(F32)
            for side in range(woven.shape[0]):
                woven[side] = g_conv[:, side * 128 : side * 128 + 128]
            part_rows(woven, first, g_conv_ref)


def feed_backward(place, g_stream, middle, gain, gate, slope, mixer_pieces, feed_pieces):
    rows, width = g_stream.shape
    part = pl.BlockSpec((rows, width), lambda j, *_: (0, j))
    whole = once((rows, width))
    return pl.pallas_call(
        feed_backward_kernel,
        grid_spec=pltpu.PrefetchScalarGridSpec(
            num_scalar_prefetch=1,
            grid=(4,),
            in_specs=[whole, whole, once((1, width)), whole, part] + [ANYWHERE] * (4 * PIECES),
            out_specs=[whole, part, whole, whole, whole, whole, once((8, width)), once((8, width))],
            scratch_shapes=[
                pltpu.VMEM((width, width), BF16),
                pltpu.VMEM((2, width, width), BF16),
                pltpu.VMEM((2, width, width), BF16),
                pltpu.VMEM((rows, width), F32),
                pltpu.VMEM((width // 128, BLOCK, 128), F32),
                pltpu.SemaphoreType.DMA,
                pltpu.SemaphoreType.DMA((2,)),
                pltpu.SemaphoreType.DMA((2,)),
            ],
        ),
        out_shape=[
            jax.ShapeDtypeStruct((rows, width), BF16),
            jax.ShapeDtypeStruct((rows, 4 * width), BF16),
            jax.ShapeDtypeStruct((rows, width), F32),
            jax.ShapeDtypeStruct((rows, width), BF16),
            jax.ShapeDtypeStruct((rows, width), BF16),
            jax.ShapeDtypeStruct((rows, width), BF16),
            jax.ShapeDtypeStruct((8, width), F32),
            jax.ShapeDtypeStruct((8, width), F32),
        ],
        compiler_params=pltpu.CompilerParams(vmem_limit_bytes=58 * MIB),
        cost_estimate=LIGHT,
        name="feed_backward",
    )(place, g_stream, middle, gain, gate, slope, *mixer_pieces, *feed_pieces)


def project_backward_kernel(place_ref, g_proj, stream, g_mid, gain, *rest):
    pieces = rest[: 2 * PIECES]
    g_stream_ref, g_gain_ref, g_bias_ref, weights, total, sem = rest[2 * PIECES :]
    rows = stream.shape[0]
    for part in range(3):
        start_columns(place_ref, pieces, 0, weights.at[part], sem, part)
    wait_whole(weights, sem)
    g_gain_ref[...] = jnp.zeros_like(g_gain_ref)
    g_bias_ref[...] = jnp.zeros_like(g_bias_ref)

    total[...] = matmul_near(g_proj[0], weights[0])
    total[...] += matmul_near(g_proj[1], weights[1])
    total[...] += matmul_near(g_proj[2], weights[2])

    def last(base):
        at = pl.ds(base, 128)
        g_normed = total[at, :]
        g_value, g_scaled = norm_backward(stream[at, :], g_normed, gain[...])
        g_stream_ref[at, :] = g_mid[at, :] + g_value
        g_gain_ref[...] += fold_rows(g_scaled)
        g_bias_ref[...] += fold_rows(g_normed)

    loop_rows(rows, 128, last)


def project_backward(place, g_proj, stream, g_mid, gain, pieces):
    rows, width = stream.shape
    whole = once((rows, width))
    return pl.pallas_call(
        project_backward_kernel,
        grid_spec=pltpu.PrefetchScalarGridSpec(
            num_scalar_prefetch=1,
            grid=(1,),
            in_specs=[once((3, rows, width)), whole, whole, once((1, width))] + [ANYWHERE] * (2 * PIECES),
            out_specs=[whole, once((8, width)), once((8, width))],
            scratch_shapes=[
                pltpu.VMEM((3, width, width), BF16),
                pltpu.VMEM((rows, width), F32),
                pltpu.SemaphoreType.DMA,
            ],
        ),
        out_shape=[
            jax.ShapeDtypeStruct((rows, width), F32),
            jax.ShapeDtypeStruct((8, width), F32),
            jax.ShapeDtypeStruct((8, width), F32),
        ],
        compiler_params=pltpu.CompilerParams(vmem_limit_bytes=48 * MIB),
        cost_estimate=LIGHT,
        name="project_backward",
    )(place, g_proj, stream, g_mid, gain, *pieces)


def strip_at(hold, z, c):
    return hold[pl.ds(strip_of(z, c), STRIP), :].astype(BF16)


def grad_up_kernel(place_ref, normed, g_pre, keep_ref, send_ref, hold):
    c = place_ref[7]
    hold[...] = matmul_lead(normed[...], g_pre[...])
    for z in range(4):
        keep_ref[0, z] = strip_at(hold, z, c)
        send_ref[0, z] = strip_at(hold, z, c ^ 1)


def grad_up(place, normed, g_pre):
    rows, width = normed.shape
    part = pl.BlockSpec((rows, width), lambda j, *_: (0, j))
    block = pl.BlockSpec((1, 4, STRIP, width), lambda j, *_: (j, 0, 0, 0))
    return pl.pallas_call(
        grad_up_kernel,
        grid_spec=pltpu.PrefetchScalarGridSpec(
            num_scalar_prefetch=1,
            grid=(4,),
            in_specs=[once((rows, width)), part],
            out_specs=[block, block],
            scratch_shapes=[pltpu.VMEM((width, width), F32)],
        ),
        out_shape=[jax.ShapeDtypeStruct((4, 4, STRIP, width), BF16)] * 2,
        compiler_params=pltpu.CompilerParams(vmem_limit_bytes=40 * MIB),
        cost_estimate=LIGHT,
        name="grad_up",
    )(place, normed, g_pre)


def grad_down_kernel(place_ref, hidden, g_down, keep_ref, send_ref, hold):
    c = place_ref[7]
    hold[...] = matmul_lead(hidden[...], g_down[...])
    for part in range(4):
        for ref, side in ((keep_ref, c), (send_ref, c ^ 1)):
            row = pl.multiple_of((side * 4 + part) * STRIP, STRIP)
            ref[part, 0] = hold[pl.ds(row, STRIP), :].astype(BF16)


def grad_down(place, hidden, g_down):
    rows, width = g_down.shape
    block = pl.BlockSpec((4, 1, STRIP, width), lambda j, *_: (0, j, 0, 0))
    return pl.pallas_call(
        grad_down_kernel,
        grid_spec=pltpu.PrefetchScalarGridSpec(
            num_scalar_prefetch=1,
            grid=(4,),
            in_specs=[pl.BlockSpec((rows, width), lambda j, *_: (0, j)), once((rows, width))],
            out_specs=[block, block],
            scratch_shapes=[pltpu.VMEM((width, width), F32)],
        ),
        out_shape=[jax.ShapeDtypeStruct((4, 4, STRIP, width), BF16)] * 2,
        compiler_params=pltpu.CompilerParams(vmem_limit_bytes=40 * MIB),
        cost_estimate=LIGHT,
        name="grad_down",
    )(place, hidden, g_down)


def grad_rows_kernel(place_ref, left, right, keep_ref, send_ref, hold):
    c = place_ref[7]
    quarter = STRIP // 4
    hold[...] = matmul_lead(left[...], right[0])
    for z in range(4):
        for ref, side in ((keep_ref, c), (send_ref, c ^ 1)):
            for part in range(4):
                row = pl.multiple_of(strip_of(z, side) + part * quarter, quarter)
                ref[part, z, 0] = hold[pl.ds(row, quarter), :].astype(BF16)


def grad_rows(place, left, right):
    count, rows, width = right.shape
    block = pl.BlockSpec((4, 4, 1, STRIP // 4, width), lambda j, *_: (0, 0, j, 0, 0))
    return pl.pallas_call(
        grad_rows_kernel,
        grid_spec=pltpu.PrefetchScalarGridSpec(
            num_scalar_prefetch=1,
            grid=(count,),
            in_specs=[once((rows, width)), pl.BlockSpec((1, rows, width), lambda j, *_: (j, 0, 0))],
            out_specs=[block, block],
            scratch_shapes=[pltpu.VMEM((width, width), F32)],
        ),
        out_shape=[jax.ShapeDtypeStruct((4, 4, count, STRIP // 4, width), BF16)] * 2,
        compiler_params=pltpu.CompilerParams(vmem_limit_bytes=40 * MIB),
        cost_estimate=LIGHT,
        name="grad_rows",
    )(place, left, right)


def order_kernel(place_ref, held_ref, out_ref):
    out_ref[...] = held_ref[0]


def in_channel_order(place, held):
    count, rows, width = held.shape
    return pl.pallas_call(
        order_kernel,
        grid_spec=pltpu.PrefetchScalarGridSpec(
            num_scalar_prefetch=1,
            grid=(count,),
            in_specs=[pl.BlockSpec((1, rows, width), lambda j, *_: (j, 0, 0))],
            out_specs=pl.BlockSpec((rows, width), lambda j, place_ref: (0, j ^ (2 * place_ref[6] + place_ref[7]))),
        ),
        out_shape=jax.ShapeDtypeStruct((rows, count * width), F32),
        cost_estimate=LIGHT,
        name="in_channel_order",
    )(place, held)


def lay_out_kernel(place_ref, ones, zero, near, side, cross, up_ref, down_ref, out_ref, in_ref):
    width = down_ref.shape[2]
    quarter = STRIP // 4
    s = place_ref[5]

    def lay(layer, part, sums):
        up_ref[layer, :, pl.ds(part * width, width)] = sums[:STRIP].astype(F32)
        down_ref[layer, pl.ds(part * STRIP, STRIP), :] = sums[STRIP : 2 * STRIP].astype(F32)
        rows = pl.ds(part * quarter, quarter)
        out_ref[layer, rows, :] = sums[2 * STRIP : 2 * STRIP + quarter].astype(F32)
        for k in range(3):
            first = 2 * STRIP + (k + 1) * quarter
            in_ref[layer, rows, pl.ds(k * width, width)] = sums[first : first + quarter].astype(F32)

    for part in range(4):
        lay(1, part, ones[part])
        for hop, source in enumerate((zero, near, side, cross)):
            pl.when((s ^ hop) == part)(functools.partial(lambda p, r: lay(0, p, r[...]), part, source))


def lay_out(place, ones, zeros):
    width = ones.shape[2]
    shapes = [(2, STRIP, 4 * width), (2, 4 * STRIP, width), (2, STRIP, width), (2, STRIP, 3 * width)]
    return pl.pallas_call(
        lay_out_kernel,
        grid_spec=pltpu.PrefetchScalarGridSpec(
            num_scalar_prefetch=1,
            grid=(1,),
            in_specs=[once(ones.shape)] + [once(zeros[0].shape)] * 4,
            out_specs=[once(shape) for shape in shapes],
        ),
        out_shape=[jax.ShapeDtypeStruct(shape, F32) for shape in shapes],
        compiler_params=pltpu.CompilerParams(vmem_limit_bytes=40 * MIB),
        cost_estimate=LIGHT,
        name="lay_out",
    )(place, ones, *zeros)


FIRST_STEPS = (((0, 2), (1, 3)), ((0, 1), (2, 3)))


def merge_kernel(place_ref, *refs, count, form):
    keeps, gots, outs = refs[:count], refs[count : 2 * count], refs[2 * count :]
    s = place_ref[5]
    for part in range(4):
        at = part if form == "whole" else s ^ part
        rows = [
            (keep[at, 0].astype(F32) + got[at, 0].astype(F32)).astype(BF16) for keep, got in zip(keeps, gots)
        ]
        rows = jnp.concatenate(rows, axis=0) if count > 1 else rows[0]
        if form == "whole":
            outs[0][part, 0] = rows
        elif form == "hops":
            outs[part][0] = rows
        else:
            half = rows.shape[0] // 2
            for side, groups in enumerate(FIRST_STEPS):
                for group, hops in enumerate(groups):
                    if part in hops:
                        outs[2 * side + group][hops.index(part), 0] = rows[side * half : side * half + half]


def merge_cores(place, keeps, gots, form):
    width = keeps[0].shape[-1]
    rows = sum(keep.shape[2] for keep in keeps)
    blocks = [pl.BlockSpec((4, 1, keep.shape[2], width), lambda j, *_: (0, j, 0, 0)) for keep in keeps]
    if form == "hops":
        out_specs = [pl.BlockSpec((1, rows, width), lambda j, *_: (j, 0, 0))] * 4
        out_shape = [jax.ShapeDtypeStruct((4, rows, width), BF16)] * 4
    elif form == "whole":
        out_specs = [pl.BlockSpec((4, 1, rows, width), lambda j, *_: (0, j, 0, 0))]
        out_shape = [jax.ShapeDtypeStruct((4, 4, rows, width), BF16)]
    else:
        out_specs = [pl.BlockSpec((2, 1, rows // 2, width), lambda j, *_: (0, j, 0, 0))] * 4
        out_shape = [jax.ShapeDtypeStruct((2, 4, rows // 2, width), BF16)] * 4
    return pl.pallas_call(
        functools.partial(merge_kernel, count=len(keeps), form=form),
        grid_spec=pltpu.PrefetchScalarGridSpec(
            num_scalar_prefetch=1, grid=(4,), in_specs=blocks * 2, out_specs=out_specs
        ),
        out_shape=out_shape,
        compiler_params=pltpu.CompilerParams(vmem_limit_bytes=40 * MIB),
        cost_estimate=LIGHT,
        name="merge_cores",
    )(place, *keeps, *gots)


def xor_pairs(count, bits):
    return [(i, i ^ bits) for i in range(count)]


def hop_pairs(chan_count, per_group, shift):
    return [
        (i, i + shift)
        for i in range(chan_count)
        if 0 <= i % per_group + shift < per_group
    ]


def across_cores(values):
    return lax.ppermute(values, "core", xor_pairs(lax.axis_size("core"), 1))


def across_line(values, hop):
    return lax.ppermute(values, "line", xor_pairs(lax.axis_size("line"), hop))


def across_plane(values, hop):
    return lax.ppermute(values, "seq", xor_pairs(lax.axis_size("seq"), hop))


def pick(values, index):
    return lax.dynamic_index_in_dim(values, index, axis=0, keepdims=False)


def barrier(*values):
    return lax.optimization_barrier(values)


def line_pieces(shard, s):
    mine = pick(shard, s)
    return [across_line(mine, hop) for hop in range(1, 4)]


def to_planes(values, hops=(1, 2, 3)):
    return [across_plane(values, hop) for hop in hops]


def in_order(held, s):
    held = jnp.stack(held)
    return jnp.stack([pick(held, s ^ part) for part in range(4)])


def add_all(first, others):
    total = first.astype(F32)
    for values in others:
        total = total + values.astype(F32)
    return total.astype(BF16)


def send_planes(parts):
    return [across_plane(parts[hop], hop) for hop in range(1, 4)]


def send_lines(values, z, hops=(1, 2, 3)):
    return [across_line(pick(values, z ^ hop), hop) for hop in hops]


def scatter_planes(values):
    return lax.psum_scatter(values, "seq", scatter_dimension=0, tiled=False)


def scatter_lines(values):
    return lax.psum_scatter(values, "line", scatter_dimension=0, tiled=False)


def share_planes(values):
    return lax.all_gather(values, "seq", axis=0)


def sum_everywhere(values):
    for send in (
        across_cores,
        lambda v: across_line(v, 1),
        lambda v: across_line(v, 2),
        lambda v: across_plane(v, 1),
        lambda v: across_plane(v, 2),
    ):
        values = values + send(values)
    return values


def gather_small(values):
    held = values[None]
    for send in (across_cores, lambda v: across_line(v, 1), lambda v: across_line(v, 2)):
        held = jnp.concatenate([held, send(held)], axis=0)
    return held


def chan_permute(values, pairs):
    return lax.ppermute(values, ("line", "core"), pairs)


def sequence_local(
    tokens_in,
    ln_gain,
    ln_bias,
    in_weight,
    short_weight,
    filter_first,
    filter_mid,
    filter_last,
    conv_bias,
    out_weight,
    up_weight,
    down_weight,
    group_kind,
    filt_len,
    decay_win,
    cotangent,
):
    chan_count = lax.axis_size("line") * lax.axis_size("core")
    seq_index = lax.axis_index("seq")
    chan_index = lax.axis_index(("line", "core"))
    local_rows, width = tokens_in.shape
    chan_width = conv_bias.shape[1]
    hid = filter_last.shape[1]
    per_group = chan_count // 2
    group_len = local_rows * per_group
    place_in = chan_index % per_group
    line_index = chan_index // 2
    group_index = 2 * seq_index + chan_index // per_group
    kind = pick(group_kind, group_index)
    stop = pick(filt_len, group_index)
    span = pick(decay_win, group_index)
    earlier = jnp.where(kind == 1, place_in, place_in % 2)
    later = jnp.where(kind == 1, per_group - 1 - place_in, 1 - place_in % 2)
    place = jnp.stack(
        [earlier, later, place_in % 2, stop, span, seq_index, line_index, chan_index % 2]
    ).astype(jnp.int32)
    dft, inverse = (jnp.asarray(table) for table in transform_tables())
    rates = jnp.exp(
        jnp.log(0.3) + jnp.log(100.0) * jnp.arange(width, dtype=jnp.int32).astype(F32) / (width - 1)
    )[None, :]
    row = jnp.arange(group_len, dtype=jnp.int32)
    positions = (row // BLOCK * BLOCK + row % HALF * 2 + row % BLOCK // HALF).astype(F32)
    features = position_features(positions, group_len)
    ahead = hop_pairs(chan_count, per_group, 2)
    back = hop_pairs(chan_count, per_group, -2)
    ahead_one = hop_pairs(chan_count, per_group, 1)
    back_one = hop_pairs(chan_count, per_group, -1)

    def neighbours(values, pairs):
        partner = across_cores(values)
        far = chan_permute(values, pairs)
        return (values, partner, far, across_cores(far))

    small = jnp.concatenate(
        [
            filter_last,
            short_weight.reshape(LAYERS, 9, chan_width),
            conv_bias[:, None, :],
            ln_gain.astype(F32),
            ln_bias.astype(F32),
        ],
        axis=1,
    )

    def mixer_shard(layer_index):
        columns = in_weight[layer_index].reshape(chan_width, 3, width).transpose(1, 0, 2)
        return jnp.concatenate([columns, out_weight[layer_index][None]])[:, None]

    def feed_shard(layer_index):
        up = up_weight[layer_index].reshape(chan_width, 4, width).transpose(1, 0, 2)
        down = down_weight[layer_index].reshape(4, chan_width, width)
        return jnp.stack([up, down], axis=1)

    def filter_acts(layer_index):
        first_act = precise_dot(features, filter_first[layer_index])
        first_sin = jnp.sin(first_act)
        middle_act = precise_dot(first_sin, filter_mid[layer_index])
        middle_sin = jnp.sin(middle_act)
        high = middle_sin.astype(BF16)
        low = (middle_sin - high.astype(F32)).astype(BF16)
        return first_act, first_sin, middle_act, jnp.concatenate([high, high, low], axis=1), high.T

    mixer_shards = [mixer_shard(layer_index) for layer_index in range(LAYERS)]
    feed_shards = [feed_shard(layer_index) for layer_index in range(LAYERS)]
    s, z = seq_index, line_index

    def line_hops(shard, hops):
        mine = pick(shard, s)
        return [across_line(mine, hop) for hop in hops]

    mixer_line = line_pieces(mixer_shards[0], s)
    feed_line = line_hops(feed_shards[0], (1,))
    mixer_line, feed_line, feed_shards[0], filter_first = barrier(mixer_line, feed_line, feed_shards[0], filter_first)

    windows = [None] * LAYERS
    small = gather_small(small.reshape(-1, chan_width))
    mixer_line = jnp.stack(mixer_line)
    mixer_plane = to_planes(mixer_line)
    feed_line = feed_line + line_hops(feed_shards[0], (2,))
    acts = [filter_acts(layer_index) for layer_index in range(LAYERS)]
    mixer_line, mixer_plane, small, acts, feed_line, place = barrier(
        mixer_line, mixer_plane, small, acts, feed_line, place
    )

    mixer_pieces, feed_pieces = [None] * LAYERS, [None] * LAYERS
    mixer_all = in_order([mixer_line, *mixer_plane], s)
    mixer_all_twin = across_cores(mixer_all)
    mixer_twin = across_cores(mixer_shards[0])
    above = chan_permute(tokens_in[-EDGE:], ahead_one)
    feed_line = feed_line + line_hops(feed_shards[0], (3,))
    small = in_channel_order(place, small).reshape(LAYERS, hid + 14, width)
    mixer_all, mixer_all_twin, mixer_twin, above, small, feed_line = barrier(
        mixer_all, mixer_all_twin, mixer_twin, above, small, feed_line
    )
    mixer_pieces[0] = [mixer_shards[0], mixer_all, mixer_twin, mixer_all_twin]
    last_all, taps_all, shift_all = small[:, :hid], small[:, hid : hid + 9], small[:, hid + 9 : hid + 10]
    gain_all, bias_all = small[:, hid + 10 : hid + 12], small[:, hid + 12 : hid + 14]

    def last_parts(i):
        high = last_all[i].astype(BF16)
        low = (last_all[i] - high.astype(F32)).astype(BF16)
        return jnp.concatenate([high, low, high], axis=0)

    stream = tokens_in
    kept = []
    for i in range(LAYERS):
        more = i + 1 < LAYERS
        if more:
            twins = [across_cores(v) for v in (feed_shards[0], mixer_shards[1])]
            feed_line = jnp.stack(feed_line)
            feed_plane = to_planes(feed_line, (1, 2))
        normed_in, *projected, edge, signal, gate = project(
            place, stream, above, gain_all[i, :1], bias_all[i, :1], taps_all[i], mixer_pieces[i]
        )
        if more:
            signal, projected, feed_line, feed_plane, twins = barrier(signal, projected, feed_line, feed_plane, twins)
        else:
            signal, projected = barrier(signal, projected)
        partner = across_cores(signal)
        far = chan_permute(signal, ahead)
        if more:
            feed_plane = feed_plane + to_planes(feed_line, (3,))
        windows[i] = window_spectra(place, acts[i][3], last_parts(i), rates, dft)
        if more:
            far, partner, feed_plane, windows[i] = barrier(far, partner, feed_plane, windows[i])
            feed_all = in_order([feed_line, *feed_plane], s)
        else:
            cosines = [(jnp.cos(acts[0][0]), jnp.cos(acts[0][2])), None]
            far, partner, feed_all, windows[i], cosines[0] = barrier(far, partner, feed_all, windows[i], cosines[0])
        beyond = across_cores(far)
        feed_all_twin = across_cores(feed_all)
        if more:
            mixer_line = line_pieces(mixer_shards[i + 1], s)
        signals = barrier(signal, partner, far, beyond)
        gated, conv = conv_forward(place, *signals, windows[i], dft, inverse, gate, shift_all[i])
        if more:
            gated, feed_all_twin, mixer_line = barrier(gated, feed_all_twin, mixer_line)
            feed_pieces[i] = [feed_shards[i], feed_all, twins[0], feed_all_twin]
            mixer_line = jnp.stack(mixer_line)
            mixer_plane = to_planes(mixer_line)
            feed_line = line_pieces(feed_shards[i + 1], s)
        else:
            gated, feed_all_twin = barrier(gated, feed_all_twin)
            feed_pieces[i] = [feed_shards[i], feed_all, twins[0], feed_all_twin]
        before = stream
        stream, middle, normed_mid, hidden, slope = feed_forward(
            place, stream, gated, gain_all[i, 1:], bias_all[i, 1:], mixer_pieces[i], feed_pieces[i]
        )
        kept.append((before, normed_in, projected, edge, signals, gate, gated, conv, middle, normed_mid, hidden, slope))
        if more:
            stream, mixer_line, mixer_plane, feed_line = barrier(stream, mixer_line, mixer_plane, feed_line)
            above = chan_permute(stream[-EDGE:], ahead_one)
            feed_all = share_planes(jnp.stack(feed_line))
            mixer_all = in_order([mixer_line, *mixer_plane], s)
            mixer_all_twin = across_cores(mixer_all)
            mixer_all, mixer_all_twin, above = barrier(mixer_all, mixer_all_twin, above)
            mixer_pieces[i + 1] = [mixer_shards[i + 1], mixer_all, twins[1], mixer_all_twin]
            twins[0] = across_cores(feed_shards[i + 1])

    def flat(part):
        return part.reshape(4, 4, -1, width)

    def small_sums(i, grads):
        grad_last, g_middle, g_taps, g_shift = grads
        first_sin = acts[i][1]
        first_cos, middle_cos = cosines[i] or (jnp.cos(acts[i][0]), jnp.cos(acts[i][2]))
        g_middle = g_middle * middle_cos
        grad_middle = lax.dot_general(
            first_sin, g_middle, (((0,), (0,)), ((), ())), precision=HIGHEST, preferred_element_type=F32
        )
        g_first = lax.dot_general(
            g_middle, filter_mid[i], (((1,), (1,)), ((), ())), precision=HIGHEST, preferred_element_type=F32
        ) * first_cos
        grad_first = lax.dot_general(
            features, g_first, (((0,), (0,)), ((), ())), precision=HIGHEST, preferred_element_type=F32
        )
        rest = jnp.concatenate([grad_first, grad_middle], axis=0).reshape(-1)
        rest = jnp.pad(rest, (0, -rest.size % width)).reshape(-1, width)
        return jnp.concatenate(
            [grad_last, jnp.sum(g_taps, axis=1), jnp.sum(g_shift, axis=0)[None], rest], axis=0
        )

    def norm_sums(*grads):
        return jnp.sum(jnp.stack(grads), axis=1)

    def backward_feed(i, g_stream):
        (_, _, _, _, _, gate, _, _, middle, _, _, slope) = kept[i]
        return feed_backward(
            place, g_stream, middle, gain_all[i, 1:], gate, slope, mixer_pieces[i], feed_pieces[i]
        )

    def backward_conv(i, g_gated, g_convs):
        (_, _, projected, edge, signals, _, _, conv, _, _, _, _) = kept[i]
        return conv_backward(
            place, signals, g_convs, windows[i], dft, inverse, projected, edge, taps_all[i], shift_all[i], g_gated,
            conv, rates, acts[i][4], last_all[i],
        )

    def mend(i, g_proj, g_ahead):
        g_ahead = jnp.where(later > 0, g_ahead, 0).astype(F32)
        taps_of = taps_all[i].reshape(3, 3, width)
        last_fix = taps_of[1] * g_ahead[:, 0] + taps_of[2] * g_ahead[:, 1]
        before_fix = taps_of[2] * g_ahead[:, 0]
        fix = jnp.concatenate(
            [jnp.zeros((3, EDGE - 2, width), F32), before_fix[:, None], last_fix[:, None]], axis=1
        )
        tail = (g_proj[:, -EDGE:].astype(F32) + fix).astype(BF16)
        return lax.dynamic_update_slice(g_proj, tail, (0, local_rows - EDGE, 0))

    def out_grads(i, g_out):
        return [flat(part) for part in grad_rows(place, kept[i][6], g_out[None])]

    g_down, g_pre, g_mid, g_out, g_gated, g_conv, g_gain_two, g_bias_two = barrier(*backward_feed(1, cotangent))
    partner = across_cores(g_conv)
    far = chan_permute(g_conv, back)
    down = grad_down(place, kept[1][10], g_down)
    up = grad_up(place, kept[1][9], g_pre)
    partner, far, down, up = barrier(partner, far, down, up)
    beyond = across_cores(far)
    out = out_grads(1, g_out)
    beyond, out = barrier(beyond, out)
    got = [across_cores(values[1]) for values in (up, down, out)]
    g_proj, g_edge, *filter_grads = backward_conv(1, g_gated, (g_conv, partner, far, beyond))
    g_proj, g_edge, got, filter_grads = barrier(g_proj, g_edge, got, filter_grads)
    g_ahead = chan_permute(g_edge, back_one)
    feed_one = merge_cores(place, (up[0], down[0]), got[:2], "whole")[0]
    g_ahead, feed_one = barrier(g_ahead, feed_one)
    feed_one = scatter_planes(feed_one)
    g_proj = mend(1, g_proj, g_ahead)
    in_one = [flat(part) for part in grad_rows(place, kept[1][1], g_proj)]
    in_one, g_proj = barrier(in_one, g_proj)
    in_got = across_cores(in_one[1])
    g_stream, g_gain_one, g_bias_one = project_backward(
        place, g_proj, kept[1][0], g_mid, gain_all[1, :1], mixer_pieces[1]
    )
    g_stream, in_got, g_gain_one, g_bias_one = barrier(g_stream, in_got, g_gain_one, g_bias_one)
    norms_one = norm_sums(g_gain_one, g_gain_two, g_bias_one, g_bias_two)
    results, feed_one = barrier(backward_feed(0, g_stream), feed_one)
    ones = merge_cores(place, (out[0], in_one[0]), (got[2], in_got), "whole")[0]
    ones, results = barrier(ones, results)
    ones = scatter_planes(ones)
    g_down, g_pre, g_mid, g_out, g_gated, g_conv, g_gain_two, g_bias_two = results
    partner = across_cores(g_conv)
    far = chan_permute(g_conv, back)
    down = grad_down(place, kept[0][10], g_down)
    small_one = jnp.concatenate([small_sums(1, filter_grads), norms_one])
    partner, far, down, small_one = barrier(partner, far, down, small_one)
    beyond = across_cores(far)
    down_got = across_cores(down[1])
    small_got = across_cores(small_one)
    up = grad_up(place, kept[0][9], g_pre)
    beyond, down_got, up, small_got, ones = barrier(beyond, down_got, up, small_got, ones)
    up_got = across_cores(up[1])
    small_one = small_one + small_got
    small_got = across_line(small_one, 1)
    out = out_grads(0, g_out)
    up_got, out, small_got = barrier(up_got, out, small_got)
    out_got = across_cores(out[1])
    small_one = small_one + small_got
    feed_zero = merge_cores(place, (up[0], down[0], out[0]), (up_got, down_got, out_got), "halves")
    feed_zero, small_one, ones = barrier(feed_zero, small_one, ones)
    ones = scatter_lines(jnp.concatenate([feed_one, ones], axis=1))
    feed_got = [across_plane(feed_zero[1], 1), across_plane(feed_zero[3], 2)]
    small_got = across_line(small_one, 2)
    g_proj, g_edge, *filter_grads = backward_conv(0, g_gated, (g_conv, partner, far, beyond))
    g_proj, g_edge, filter_grads, small_got, ones, feed_got = barrier(
        g_proj, g_edge, filter_grads, small_got, ones, feed_got
    )
    ones = share_planes(ones)
    feed_sent = [add_all(feed_zero[2 * side][1], [feed_got[side][1]]) for side in range(2)]
    last_got = [across_plane(feed_sent[0], 2), across_plane(feed_sent[1], 1)]
    g_ahead = chan_permute(g_edge, back_one)
    small_one = small_one + small_got
    g_ahead, small_one = barrier(g_ahead, small_one)
    small_got = across_plane(small_one, 1)
    g_proj = mend(0, g_proj, g_ahead)
    in_zero = [flat(part) for part in grad_rows(place, kept[0][1], g_proj)]
    in_zero, g_proj, small_got, last_got = barrier(in_zero, g_proj, small_got, last_got)
    in_got = across_cores(in_zero[1])
    small_one = small_one + small_got
    small_zero = small_sums(0, filter_grads)
    small_zero, in_got, small_one, g_proj = barrier(small_zero, in_got, small_one, g_proj)
    feed_zero = jnp.concatenate(
        [add_all(feed_zero[2 * side][0], [feed_got[side][0], last_got[side]]) for side in range(2)], axis=1
    )
    feed_got = send_lines(feed_zero, z, (1,))
    in_zero = merge_cores(place, in_zero[:1], [in_got], "hops")
    in_zero, feed_zero, g_proj, feed_got = barrier(in_zero, feed_zero, g_proj, feed_got)
    in_got = send_planes(in_zero)
    feed_got = feed_got + send_lines(feed_zero, z, (2,))
    small_got = across_cores(small_zero)
    g_stream, g_gain_one, g_bias_one = project_backward(
        place, g_proj, kept[0][0], g_mid, gain_all[0, :1], mixer_pieces[0]
    )
    g_stream, g_gain_one, g_bias_one, in_got, feed_got, small_got = barrier(
        g_stream, g_gain_one, g_bias_one, in_got, feed_got, small_got
    )
    in_zero = add_all(in_zero[0], in_got)
    in_got = send_lines(in_zero, z)
    feed_got = feed_got + send_lines(feed_zero, z, (3,))
    norms = norm_sums(g_gain_one, g_gain_two, g_bias_one, g_bias_two)
    norms = norms + across_cores(norms)
    small_zero = jnp.concatenate([small_zero + small_got, norms])
    feed_got, in_got, small_zero = barrier(feed_got, in_got, small_zero)
    feed_zero = add_all(pick(feed_zero, z), feed_got)
    in_zero = add_all(pick(in_zero, z), in_got)
    zeros = jnp.concatenate([feed_zero, in_zero])
    zeros_got = to_planes(zeros)
    small_one = small_one + across_plane(small_one, 2)
    small_zero = small_zero + across_line(small_zero, 1)
    small_zero = small_zero + across_line(small_zero, 2)
    small_zero = small_zero + across_plane(small_zero, 1)
    small_zero, zeros_got, small_one = barrier(small_zero, zeros_got, small_one)
    small_got = across_plane(small_zero, 2)
    grad_up_all, grad_down_all, grad_out_all, grad_in_all = lay_out(place, ones, [zeros, *zeros_got])
    grad_up_all, small_got = barrier(grad_up_all, small_got)
    wide = jnp.stack([small_zero + small_got, small_one])
    mine = lax.dynamic_slice_in_dim(wide, chan_index * chan_width, chan_width, axis=2)
    rest = wide[:, hid + 10 : -4].reshape(LAYERS, -1)
    first_size = filter_first.shape[1] * hid
    return (
        stream,
        g_stream,
        mine[:, -4:-2],
        mine[:, -2:],
        grad_in_all,
        mine[:, hid : hid + 9].reshape(LAYERS, 3, 3, chan_width),
        rest[:, :first_size].reshape(filter_first.shape),
        rest[:, first_size : first_size + hid * hid].reshape(filter_mid.shape),
        mine[:, :hid],
        mine[:, hid + 9],
        grad_out_all,
        grad_up_all,
        grad_down_all,
    )


def fits_sequence_form(mesh):
    return mesh.shape["chan"] == 8 and mesh.shape["seq"] == 4


def solution(mesh):
    body, chan = local, "chan"
    if fits_sequence_form(mesh):
        body, chan = sequence_local, ("line", "core")
        mesh = Mesh(mesh.devices.reshape(4, 4, 2), ("seq", "line", "core"))
    rows = ("seq", *chan) if body is sequence_local else ("seq", chan)
    in_specs = (
        P(rows, None),
        P(None, None, chan),
        P(None, None, chan),
        P(None, chan, None),
        P(None, None, None, chan),
        P(),
        P(),
        P(None, None, chan),
        P(None, chan),
        P(None, chan, None),
        P(None, chan, None),
        P(None, chan, None),
        P(),
        P(),
        P(),
        P(rows, None),
    )
    out_specs = (
        P(rows, None),
        P(rows, None),
        P(None, None, chan),
        P(None, None, chan),
        P(None, chan, None),
        P(None, None, None, chan),
        P(),
        P(),
        P(None, None, chan),
        P(None, chan),
        P(None, chan, None),
        P(None, chan, None),
        P(None, chan, None),
    )
    return jax.shard_map(body, mesh=mesh, in_specs=in_specs, out_specs=out_specs, check_vma=False)
```
